32 devices in a mesh: row: 8 (over y, x, core), col: 4 (over z).
Axes of the slice: x: 2, y: 2, z: 4, core: 2. Of those that a mesh axis runs over, the one named last changes fastest.
Arguments:
- features: bfloat16 [8192, 128], P(('row', 'col')), may hold values from -6 to 6
- weight: bfloat16 [128, 128], replicated, may hold values from -0.5 to 0.5
- bias: float32 [128], replicated, may hold values from -3 to 3
- node_scale: float32 [8192], P(('row', 'col')), may hold values from 0.04 to 0.2
- cotangent: bfloat16 [8192, 128], P(('row', 'col')), may hold values from -6 to 6
- tile_row: int32 [8, 4, 8], P('row', 'col'), may hold values from 0 to 3
- tile_col: int32 [8, 4, 8], P('row', 'col'), may hold values from 0 to 7
- tile_count: int32 [8, 4], P('row', 'col'), may hold values from 1 to 8, as said below
- tile_values: bfloat16 [8, 4, 8, 256, 256], P('row', 'col'), may hold values from 0 to 1
Outputs:
- activated: bfloat16 [8192, 128], P(('row', 'col'))
- feature_grad: bfloat16 [8192, 128], P(('row', 'col'))
- weight_grad: float32 [128, 128], replicated
- bias_grad: float32 [128], replicated
The draws below stay inside these ranges and needn't reach their ends.
Inputs may be any that keep to these rules, and one draw needn't show every extreme that they name: `tile_count`: slots from this count on are ignored; in every draw some device has exactly 8 live slots.
All inputs are finite; a program needn't handle non-finite values.
Results may differ from the reference program's by a relative error of at most 0.015.
Values may be sent and summed in bfloat16 or wider, within the bound.
A program may use at most 64 MiB of HBM per device.

```python
import math
import jax
import jax.numpy as jnp
from jax import lax

F = 128
BLOCK = 256
BPD = 1
TMAX = 8
NODES = 8192
ROWBLK = 4
COLBLK = 8
N_ROW = 8
N_COL = 4


def draw_tile_count(key, part):
    key = jax.random.fold_in(key, 7)
    first, second, third = jax.random.split(key, 3)
    counts = jax.random.randint(first, (N_ROW, N_COL), max(1, TMAX // 4), TMAX + 1)
    row_pick = jax.random.randint(second, (), 0, N_ROW)
    col_pick = jax.random.randint(third, (), 0, N_COL)
    return counts.at[row_pick, col_pick].set(TMAX).astype(jnp.int32)


def place_ends(entries, key, least, largest):
    index_at = [jax.random.randint(jax.random.fold_in(key, axis), (), 0, length) for axis, length in enumerate(entries.shape)]
    main_axis = entries.shape.index(max(entries.shape))
    beside = index_at[:main_axis] + [(index_at[main_axis] + 1) % entries.shape[main_axis]] + index_at[main_axis + 1:]
    return entries.at[tuple(index_at)].set(least).at[tuple(beside)].set(largest)


def steps_of(key, extent, pieces, least, high):
    def one(dim, shards_of):
        draws = jax.random.uniform(jax.random.fold_in(jax.random.fold_in(key, 6), dim), (shards_of,), jnp.float32, least / len(pieces), high / len(pieces))
        return jnp.repeat(jnp.exp(draws), extent[dim] // shards_of).reshape((-1,) + (1,) * (len(extent) - dim - 1))

    factor_of = one(*pieces[0])
    for cut in pieces[1:]:
        factor_of = factor_of * one(*cut)
    return factor_of


def centred(rng, extent, scale, bound, cuts=(), kind=jnp.bfloat16):
    values = scale * jax.random.normal(rng, extent, jnp.float32)
    if cuts:
        values = values * steps_of(rng, extent, cuts, -0.22, 0.18)
    return jnp.clip(values, -bound, bound).astype(kind)


def setup_inputs(seed: int = 0) -> dict:
    splits = jax.random.split(jax.random.key(seed), 10)
    features = centred(splits[0], (NODES, F), 1.0, 6.0, ((0, 32),))
    weight = centred(splits[1], (F, F), F ** -0.5, 0.5)
    bias = centred(splits[2], (F,), 0.5, 3.0, (), jnp.float32)
    node_scale = jnp.clip(jnp.exp(math.log(0.2) - 1.609438 * jax.random.uniform(splits[3], (NODES,), jnp.float32) ** steps_of(splits[3], (NODES,), ((0, 32),), -0.2, 0.2)), 0.04, 0.2)
    cotangent = centred(splits[4], (NODES, F), 1.0, 6.0, ((0, 32),))
    tile_row = place_ends(jax.random.randint(splits[5], (N_ROW, N_COL, TMAX), 0, ROWBLK), jax.random.fold_in(splits[5], 1), 0, ROWBLK - 1).astype(jnp.int32)
    tile_col = place_ends(jax.random.randint(splits[6], (N_ROW, N_COL, TMAX), 0, COLBLK), jax.random.fold_in(splits[6], 1), 0, COLBLK - 1).astype(jnp.int32)
    tile_count = draw_tile_count(jax.random.fold_in(splits[9], 71), 0)
    tile_values = jnp.clip(1.0 * jax.random.uniform(splits[8], (N_ROW, N_COL, TMAX, BLOCK, BLOCK), jnp.float32) ** steps_of(splits[8], (N_ROW, N_COL, TMAX, BLOCK, BLOCK), ((0, 8), (1, 4)), -0.2, 0.2), 0.0, 1.0).astype(jnp.bfloat16)
    return {"features": features, "weight": weight, "bias": bias, "node_scale": node_scale, "cotangent": cotangent, "tile_row": tile_row, "tile_col": tile_col, "tile_count": tile_count, "tile_values": tile_values}


def device_partials(x_five, tile_row, tile_col, tile_count, tile_values, dev):
    r = dev // N_COL
    c = dev % N_COL
    nbr = N_COL * BPD
    nbc = N_ROW * BPD
    x_rows = lax.dynamic_index_in_dim(x_five, r, 0, keepdims=False).reshape(nbr, BLOCK, F)
    x_cols = lax.dynamic_index_in_dim(x_five, c, 1, keepdims=False).reshape(nbc, BLOCK, F)
    rows_idx = tile_row[r, c]
    cols_idx = tile_col[r, c]
    count = tile_count[r, c]
    tiles = tile_values[r, c].astype(jnp.float32)
    slots = jnp.arange(TMAX, dtype=jnp.int32)
    glob_i = r * nbr + rows_idx
    glob_j = ((cols_idx // BPD) * N_COL + c) * BPD + cols_idx % BPD
    weights = jnp.where(slots < count, jnp.where(glob_i == glob_j, 0.5, 1.0), 0.0).astype(jnp.float32)
    row_hot = (jnp.arange(nbr, dtype=jnp.int32)[:, None] == rows_idx[None, :]).astype(jnp.float32) * weights[None, :]
    col_hot = (jnp.arange(nbc, dtype=jnp.int32)[:, None] == cols_idx[None, :]).astype(jnp.float32) * weights[None, :]
    row_terms = jnp.einsum("tab,tbf->taf", tiles, x_cols[cols_idx].astype(jnp.float32))
    col_terms = jnp.einsum("tab,taf->tbf", tiles, x_rows[rows_idx].astype(jnp.float32))
    row_part = jnp.einsum("it,taf->iaf", row_hot, row_terms).astype(jnp.bfloat16)
    col_part = jnp.einsum("jt,tbf->jbf", col_hot, col_terms).astype(jnp.bfloat16)
    return r, c, row_part, col_part


def aggregate(blocks, tile_row, tile_col, tile_count, tile_values):
    x_five = blocks.reshape(N_ROW, N_COL, BPD, BLOCK, F)

    def step(total, dev):
        r, c, row_part, col_part = device_partials(x_five, tile_row, tile_col, tile_count, tile_values, dev)
        row_slab = lax.dynamic_index_in_dim(total, r, 0, keepdims=False)
        row_slab = row_slab + row_part.astype(jnp.float32).reshape(N_COL, BPD, BLOCK, F)
        total = lax.dynamic_update_index_in_dim(total, row_slab, r, 0)
        col_slab = lax.dynamic_index_in_dim(total, c, 1, keepdims=False)
        col_slab = col_slab + col_part.astype(jnp.float32).reshape(N_ROW, BPD, BLOCK, F)
        total = lax.dynamic_update_index_in_dim(total, col_slab, c, 1)
        return total, None

    start = jnp.zeros((N_ROW, N_COL, BPD, BLOCK, F), jnp.float32)
    total, unused = lax.scan(step, start, jnp.arange(N_ROW * N_COL, dtype=jnp.int32))
    return total.reshape(NODES, F)


def reference(features, weight, bias, node_scale, cotangent, tile_row, tile_col, tile_count, tile_values):
    scale = node_scale[:, None]
    projected = (scale * jnp.dot(features, weight, preferred_element_type=jnp.float32)).astype(jnp.bfloat16)
    summed = aggregate(projected, tile_row, tile_col, tile_count, tile_values)
    preact = scale * (summed + projected.astype(jnp.float32)) + bias[None, :]
    activated = jax.nn.silu(preact).astype(jnp.bfloat16)
    sig = jax.nn.sigmoid(preact)
    delta = cotangent.astype(jnp.float32) * sig * (1.0 + preact * (1.0 - sig))
    scaled_delta = (scale * delta).astype(jnp.bfloat16)
    back = aggregate(scaled_delta, tile_row, tile_col, tile_count, tile_values)
    proj_grad = (scale * (back + scaled_delta.astype(jnp.float32))).astype(jnp.bfloat16)
    feature_grad = jnp.dot(proj_grad, weight.T, preferred_element_type=jnp.float32).astype(jnp.bfloat16)
    weight_grad = jnp.dot(features.T, proj_grad, preferred_element_type=jnp.float32)
    bias_grad = jnp.sum(delta, axis=0)
    return activated, feature_grad, weight_grad, bias_grad
```

```python
import functools

import jax
import jax.numpy as jnp
from jax import lax
from jax.experimental import pallas as pl
from jax.experimental.pallas import tpu as pltpu
from jax.sharding import PartitionSpec as P

BLOCK = 256
MESH = pl.DeviceIdType.MESH
F32 = jnp.float32
BF16 = jnp.bfloat16


def dot(a, b, dims=((1,), (0,))):
    return lax.dot_general(a, b, (dims, ((), ())), preferred_element_type=F32)


def layer_kernel(
    n_row, n_col, slots,
    rows_ref, cols_ref, count_ref, features_ref, weight_ref, bias_ref, scale_ref, cotangent_ref,
    tiles_hbm,
    act_ref, fgrad_ref, wgrad_ref, bgrad_ref,
    tiles, tiles_t, scale, terms, x_row0, x_row1, x_col0, x_col1, out_row, out_col, in_row, in_col,
    w_part, w_in, w_cross, w_all, load_sem, send_sem, recv_sem,
):
    r = lax.axis_index("row")
    c = lax.axis_index("col")
    width = features_ref.shape[1]
    chunk = width // n_row

    load = pltpu.make_async_copy(tiles_hbm, tiles, load_sem)
    load.start()

    row_peers = [lax.rem(r + k, n_row) for k in range(n_row)]
    col_peers = [lax.rem(c + k, n_col) for k in range(n_col)]

    barrier = pltpu.get_barrier_semaphore()
    for peer in row_peers[1:]:
        pl.semaphore_signal(barrier, inc=1, device_id=(peer, c), device_id_type=MESH)
    for peer in col_peers[1:]:
        pl.semaphore_signal(barrier, inc=1, device_id=(r, peer), device_id_type=MESH)

    def send_along_row(stage, k, src, dst):
        copy = pltpu.make_async_remote_copy(
            src_ref=src, dst_ref=dst.at[r],
            send_sem=send_sem.at[stage, k], recv_sem=recv_sem.at[stage, r],
            device_id=(row_peers[k], c), device_id_type=MESH)
        copy.start()
        sent.append(copy)

    def send_along_col(stage, k, src, dst):
        copy = pltpu.make_async_remote_copy(
            src_ref=src, dst_ref=dst.at[c],
            send_sem=send_sem.at[stage, n_row + k], recv_sem=recv_sem.at[stage, n_row + c],
            device_id=(r, col_peers[k]), device_id_type=MESH)
        copy.start()
        sent.append(copy)

    def wait_row(stage, dst, k):
        peer = row_peers[k]
        pltpu.make_async_remote_copy(
            src_ref=dst.at[peer], dst_ref=dst.at[peer],
            send_sem=send_sem.at[stage, k], recv_sem=recv_sem.at[stage, peer],
            device_id=(peer, c), device_id_type=MESH).wait_recv()

    def wait_col(stage, dst, k):
        peer = col_peers[k]
        pltpu.make_async_remote_copy(
            src_ref=dst.at[peer], dst_ref=dst.at[peer],
            send_sem=send_sem.at[stage, n_row + k], recv_sem=recv_sem.at[stage, n_row + peer],
            device_id=(r, peer), device_id_type=MESH).wait_recv()

    sent = []
    x_row = (x_row0, x_row1)
    x_col = (x_col0, x_col1)

    def gather(phase, block):
        xr, xc = x_row[phase], x_col[phase]
        xr[c] = block
        xc[r] = block
        if phase == 0:
            pl.semaphore_wait(barrier, n_row + n_col - 2)
        for k in range(1, max(n_row, n_col)):
            if k < n_row:
                send_along_row(phase, k, xc.at[r], xc)
            if k < n_col:
                send_along_col(phase, k, xr.at[c], xr)

    row_at = [rows_ref[t] for t in range(slots)]
    col_at = [cols_ref[t] for t in range(slots)]
    count = count_ref[0]
    weights = [
        jnp.where(
            t < count,
            jnp.where(r * n_col + row_at[t] == col_at[t] * n_col + c, 0.5, 1.0),
            0.0,
        ).astype(F32)
        for t in range(slots)
    ]

    def partial(at, index):
        total = None
        for t in range(slots):
            term = terms[t] * jnp.where(at[t] == index, weights[t], 0.0)
            total = term if total is None else total + term
        return total.astype(BF16)

    def spread(phase):
        xr, xc = x_row[phase], x_col[phase]
        for k in range(1, n_col):
            wait_col(phase, xr, k)
        for t in range(slots):
            terms[t] = dot(tiles_t[t], xr[row_at[t]])
        for k in range(1, n_row):
            out_col[phase, k] = partial(col_at, row_peers[k])
            send_along_row(2 + phase, k, out_col.at[phase, k], in_col.at[phase])
        in_col[phase, r] = partial(col_at, r)
        for k in range(1, n_row):
            wait_row(phase, xc, k)
        for t in range(slots):
            terms[t] = dot(tiles[t], xc[col_at[t]])
        for k in range(1, n_col):
            out_row[phase, k] = partial(row_at, col_peers[k])
            send_along_col(2 + phase, k, out_row.at[phase, k], in_row.at[phase])
        in_row[phase, c] = partial(row_at, c)

    def collect(phase, own):
        for k in range(1, n_row):
            wait_row(2 + phase, in_col.at[phase], k)
        for k in range(1, n_col):
            wait_col(2 + phase, in_row.at[phase], k)
        total = own
        for k in range(n_row):
            total = total + in_col[phase, k].astype(F32)
        for k in range(n_col):
            total = total + in_row[phase, k].astype(F32)
        return total

    scale[...] = jnp.broadcast_to(scale_ref[...], (width, BLOCK)).T
    scaled = (scale[...] * features_ref[...].astype(F32)).astype(BF16)
    gather(0, scaled)
    load.wait()
    for t in range(slots):
        tiles_t[t] = tiles[t].T
    spread(0)
    mixed = collect(0, scaled.astype(F32))
    high = mixed.astype(BF16)
    low = (mixed - high.astype(F32)).astype(BF16)
    product = dot(high, weight_ref[...]) + dot(low, weight_ref[...])
    preact = scale[...] * product + bias_ref[...]
    sig = 1.0 / (1.0 + jnp.exp(-preact))
    delta = cotangent_ref[...].astype(F32) * sig * (1.0 + preact * (1.0 - sig))
    scaled_delta = (scale[...] * delta).astype(BF16)
    gather(1, scaled_delta)
    act_ref[...] = (preact * sig).astype(BF16)

    local = dot(high, scaled_delta, ((0,), (0,)))
    local_bias = jnp.sum(delta, axis=0, keepdims=True)
    for k in range(n_row):
        w_part[k, :chunk, :] = local[k * chunk:(k + 1) * chunk]
        w_part[k, chunk:, :] = jnp.broadcast_to(local_bias, (8, width))
    for k in range(1, n_row):
        send_along_row(4, k, w_part.at[row_peers[k]], w_in)
    w_in[r] = w_part[r]
    for k in range(1, n_row):
        wait_row(4, w_in, k)
    summed = w_in[0]
    for k in range(1, n_row):
        summed = summed + w_in[k]
    w_cross[c] = summed
    for k in range(1, n_col):
        send_along_col(4, k, w_cross.at[c], w_cross)
    spread(1)
    for k in range(1, n_col):
        wait_col(4, w_cross, k)
    summed = w_cross[0]
    for k in range(1, n_col):
        summed = summed + w_cross[k]
    w_all[r] = summed
    for k in range(1, n_row):
        send_along_row(5, k, w_all.at[r], w_all)
    bgrad_ref[...] = summed[chunk:chunk + 1]

    back = collect(1, scaled_delta.astype(F32))
    proj_grad = (scale[...] * back).astype(BF16)
    fgrad_ref[...] = dot(proj_grad, weight_ref[...], ((1,), (1,))).astype(BF16)
    for k in range(1, n_row):
        wait_row(5, w_all, k)
    for k in range(n_row):
        wgrad_ref[k * chunk:(k + 1) * chunk, :] = w_all[k, :chunk, :]
    for copy in sent:
        copy.wait_send()


def shards(
    n_row, n_col,
    features, weight, bias, node_scale, cotangent, tile_row, tile_col, tile_count, tile_values
):
    width = features.shape[1]
    slots = tile_row.shape[-1]
    assert features.shape[0] == BLOCK
    chunk = width // n_row
    vmem = pl.BlockSpec(memory_space=pltpu.VMEM)
    smem = pl.BlockSpec(memory_space=pltpu.SMEM)
    peers = n_row + n_col
    act, fgrad, wgrad, bgrad = pl.pallas_call(
        functools.partial(layer_kernel, n_row, n_col, slots),
        out_shape=(
            jax.ShapeDtypeStruct((BLOCK, width), BF16),
            jax.ShapeDtypeStruct((BLOCK, width), BF16),
            jax.ShapeDtypeStruct((width, width), F32),
            jax.ShapeDtypeStruct((1, width), F32),
        ),
        in_specs=[smem, smem, smem, vmem, vmem, vmem, vmem, vmem, pl.BlockSpec(memory_space=pl.ANY)],
        out_specs=(vmem, vmem, vmem, vmem),
        scratch_shapes=[
            pltpu.VMEM((slots, BLOCK, BLOCK), BF16),
            pltpu.VMEM((slots, BLOCK, BLOCK), BF16),
            pltpu.VMEM((BLOCK, width), F32),
            pltpu.VMEM((slots, BLOCK, width), F32),
            pltpu.VMEM((n_col, BLOCK, width), BF16),
            pltpu.VMEM((n_col, BLOCK, width), BF16),
            pltpu.VMEM((n_row, BLOCK, width), BF16),
            pltpu.VMEM((n_row, BLOCK, width), BF16),
            pltpu.VMEM((2, n_col, BLOCK, width), BF16),
            pltpu.VMEM((2, n_row, BLOCK, width), BF16),
            pltpu.VMEM((2, n_col, BLOCK, width), BF16),
            pltpu.VMEM((2, n_row, BLOCK, width), BF16),
            pltpu.VMEM((n_row, chunk + 8, width), F32),
            pltpu.VMEM((n_row, chunk + 8, width), F32),
            pltpu.VMEM((n_col, chunk + 8, width), F32),
            pltpu.VMEM((n_row, chunk + 8, width), F32),
            pltpu.SemaphoreType.DMA,
            pltpu.SemaphoreType.DMA((6, peers)),
            pltpu.SemaphoreType.DMA((6, peers)),
        ],
        compiler_params=pltpu.CompilerParams(
            collective_id=0, has_side_effects=True, vmem_limit_bytes=48 * 1024 * 1024
        ),
    )(
        tile_row.reshape(slots), tile_col.reshape(slots), tile_count.reshape(1),
        features, weight, bias.reshape(1, width), node_scale.reshape(1, BLOCK), cotangent,
        tile_values.reshape(slots, BLOCK, BLOCK),
    )
    return act, fgrad, wgrad, bgrad.reshape(width)


def solution(mesh):
    placed = (
        P(("row", "col"), None),
        P(),
        P(),
        P(("row", "col")),
        P(("row", "col"), None),
        P("row", "col", None),
        P("row", "col", None),
        P("row", "col"),
        P("row", "col", None, None, None),
    )
    return jax.shard_map(
        functools.partial(shards, mesh.shape["row"], mesh.shape["col"]),
        mesh=mesh,
        in_specs=placed,
        out_specs=(P(("row", "col"), None), P(("row", "col"), None), P(), P()),
        check_vma=False,
    )
```

```python
import functools

import jax
import jax.numpy as jnp
from jax import lax
from jax.experimental import pallas as pl
from jax.experimental.pallas import tpu as pltpu
from jax.sharding import PartitionSpec as P

BLOCK = 256
VMEM_LIMIT = 60 * 1024 * 1024
MESH = pl.DeviceIdType.MESH
F32 = jnp.float32
BF16 = jnp.bfloat16


def dot(a, b, dims=((1,), (0,))):
    return lax.dot_general(a, b, (dims, ((), ())), preferred_element_type=F32)


def layer_kernel(
    n_row, n_col, slots, halves,
    rows_hbm, cols_hbm, count_hbm, features_hbm, weight_hbm, bias_hbm, scale_hbm, cotangent_hbm,
    tiles_hbm,
    act_hbm, fgrad_hbm, wgrad_hbm, bgrad_hbm,
    act_ref, fgrad_ref, wgrad_ref, bgrad_ref, store_sem, rows_ref, cols_ref, count_ref, features, weight, bias, scale_ref, cotangent,
    tiles, tiles_t, terms, out_row, out_col, in_row, in_col,
    w_part, w_in, w_cross, w_all, load_sem, send_sem, recv_sem, *blocks,
):
    r = lax.axis_index("row")
    c = lax.axis_index("col")
    width = features.shape[1]
    chunk = width // n_row
    part = width // halves

    pairs = (
        (features_hbm, features), (scale_hbm, scale_ref), (rows_hbm, rows_ref), (cols_hbm, cols_ref),
        (count_hbm, count_ref), (tiles_hbm, tiles), (weight_hbm, weight), (bias_hbm, bias),
        (cotangent_hbm, cotangent),
    )
    loads = [pltpu.make_async_copy(src, dst, load_sem.at[n]) for n, (src, dst) in enumerate(pairs)]
    for load in loads:
        load.start()

    row_peers = [lax.rem(r + k, n_row) for k in range(n_row)]
    col_peers = [lax.rem(c + k, n_col) for k in range(n_col)]

    barrier = pltpu.get_barrier_semaphore()
    for peer in row_peers[1:]:
        pl.semaphore_signal(barrier, inc=1, device_id=(peer, c), device_id_type=MESH)
    for peer in col_peers[1:]:
        pl.semaphore_signal(barrier, inc=1, device_id=(r, peer), device_id_type=MESH)

    sent = []

    def store(n, src, dst):
        copy = pltpu.make_async_copy(src, dst, store_sem.at[n])
        copy.start()
        stores.append(copy)

    stores = []

    def send_along_row(stage, k, src, dst):
        copy = pltpu.make_async_remote_copy(
            src_ref=src, dst_ref=dst.at[r],
            send_sem=send_sem.at[stage, k], recv_sem=recv_sem.at[stage, r],
            device_id=(row_peers[k], c), device_id_type=MESH)
        copy.start()
        sent.append(copy)

    def send_along_col(stage, k, src, dst):
        copy = pltpu.make_async_remote_copy(
            src_ref=src, dst_ref=dst.at[c],
            send_sem=send_sem.at[stage, n_row + k], recv_sem=recv_sem.at[stage, n_row + c],
            device_id=(r, col_peers[k]), device_id_type=MESH)
        copy.start()
        sent.append(copy)

    def wait_row(stage, dst, k):
        peer = row_peers[k]
        pltpu.make_async_remote_copy(
            src_ref=dst.at[peer], dst_ref=dst.at[peer],
            send_sem=send_sem.at[stage, k], recv_sem=recv_sem.at[stage, peer],
            device_id=(peer, c), device_id_type=MESH).wait_recv()

    def wait_col(stage, dst, k):
        peer = col_peers[k]
        pltpu.make_async_remote_copy(
            src_ref=dst.at[peer], dst_ref=dst.at[peer],
            send_sem=send_sem.at[stage, n_row + k], recv_sem=recv_sem.at[stage, n_row + peer],
            device_id=(r, peer), device_id_type=MESH).wait_recv()

    x_row = blocks[: 2 * halves]
    x_col = blocks[2 * halves:]
    spread_at = 2 * halves
    sum_at = 4 * halves

    def gather(step, block):
        xr, xc = x_row[step], x_col[step]
        xr[c] = block
        xc[r] = block
        if step == 0:
            pl.semaphore_wait(barrier, n_row + n_col - 2)
        for k in range(1, max(n_row, n_col)):
            if k < n_col:
                send_along_col(step, k, xr.at[c], xr)
            if k < n_row:
                send_along_row(step, k, xc.at[r], xc)

    def partial(at, index, weights):
        total = None
        for t in range(slots):
            term = terms[t] * jnp.where(at[t] == index, weights[t], 0.0)
            total = term if total is None else total + term
        return total.astype(BF16)

    def spread(step, row_at, col_at, weights):
        xr, xc = x_row[step], x_col[step]
        for k in range(1, n_col):
            wait_col(step, xr, k)
        for t in range(slots):
            terms[t] = dot(xr[row_at[t]], tiles[t])
        for k in range(1, n_row):
            out_col[step, k] = partial(col_at, row_peers[k], weights)
            send_along_row(spread_at + step, k, out_col.at[step, k], in_col.at[step])
        in_col[step, r] = partial(col_at, r, weights)
        for k in range(1, n_row):
            wait_row(step, xc, k)
        for t in range(slots):
            terms[t] = dot(xc[col_at[t]], tiles_t[t])
        for k in range(1, n_col):
            out_row[step, k] = partial(row_at, col_peers[k], weights)
            send_along_col(spread_at + step, k, out_row.at[step, k], in_row.at[step])
        in_row[step, c] = partial(row_at, c, weights)

    def collect(step, own):
        for k in range(1, n_row):
            wait_row(spread_at + step, in_col.at[step], k)
        for k in range(1, n_col):
            wait_col(spread_at + step, in_row.at[step], k)
        total = own.astype(F32)
        for k in range(n_row):
            total = total + in_col[step, k].astype(F32)
        for k in range(n_col):
            total = total + in_row[step, k].astype(F32)
        return total

    for load in loads[:2]:
        load.wait()
    scale = scale_ref[...]
    scaled = (scale * features[...].astype(F32).T).astype(BF16)
    for h in range(halves):
        gather(h, scaled[h * part:(h + 1) * part])
    for load in loads[2:]:
        load.wait()
    row_at = [rows_ref[t] for t in range(slots)]
    col_at = [cols_ref[t] for t in range(slots)]
    count = count_ref[0]
    weights = [
        jnp.where(
            t < count,
            jnp.where(r * n_col + row_at[t] == col_at[t] * n_col + c, 0.5, 1.0),
            0.0,
        ).astype(F32)
        for t in range(slots)
    ]
    for t in range(slots):
        tiles_t[t] = tiles[t].T
    for h in range(halves):
        spread(h, row_at, col_at, weights)
    mixed = jnp.concatenate(
        [collect(h, scaled[h * part:(h + 1) * part]) for h in range(halves)], axis=0)
    high = mixed.astype(BF16)
    low = (mixed - high.astype(F32)).astype(BF16)
    weight_t = weight[...].T
    bias_t = jnp.broadcast_to(bias[...], (BLOCK, width)).T
    cotangent_t = cotangent[...].astype(F32).T
    acts, deltas, scaled_deltas = [], [], []
    for h in range(halves):
        rows = slice(h * part, (h + 1) * part)
        product = dot(weight_t[rows], high) + dot(weight_t[rows], low)
        preact = scale * product + bias_t[rows]
        sig = 1.0 / (1.0 + jnp.exp(-preact))
        delta = cotangent_t[rows] * sig * (1.0 + preact * (1.0 - sig))
        scaled_delta = (scale * delta).astype(BF16)
        gather(halves + h, scaled_delta)
        acts.append(preact * sig)
        deltas.append(delta)
        scaled_deltas.append(scaled_delta)

    local = dot(high, jnp.concatenate(scaled_deltas, axis=0), ((1,), (1,)))
    local_bias = jnp.sum(jnp.concatenate(deltas, axis=0).T, axis=0, keepdims=True)
    for k in range(n_row):
        w_part[k, :chunk, :] = local[k * chunk:(k + 1) * chunk]
        w_part[k, chunk:, :] = jnp.broadcast_to(local_bias, (8, width))
    for k in range(1, n_row):
        send_along_row(sum_at, k, w_part.at[row_peers[k]], w_in)
    w_in[r] = w_part[r]
    act_ref[...] = jnp.concatenate(acts, axis=0).T.astype(BF16)
    store(0, act_ref, act_hbm)
    for h in range(halves - 1):
        spread(halves + h, row_at, col_at, weights)
    for k in range(1, n_row):
        wait_row(sum_at, w_in, k)
    summed = w_in[0]
    for k in range(1, n_row):
        summed = summed + w_in[k]
    w_cross[c] = summed
    for k in range(1, n_col):
        send_along_col(sum_at, k, w_cross.at[c], w_cross)
    spread(2 * halves - 1, row_at, col_at, weights)
    for k in range(1, n_col):
        wait_col(sum_at, w_cross, k)
    summed = w_cross[0]
    for k in range(1, n_col):
        summed = summed + w_cross[k]
    w_all[r] = summed
    for k in range(1, n_row):
        send_along_row(sum_at + 1, k, w_all.at[r], w_all)
    bgrad_ref[...] = summed[chunk:chunk + 1]
    store(3, bgrad_ref, bgrad_hbm)

    fgrad_t = None
    for h in range(halves):
        proj_grad = (scale * collect(halves + h, scaled_deltas[h])).astype(BF16)
        term = dot(weight[:, h * part:(h + 1) * part], proj_grad)
        fgrad_t = term if fgrad_t is None else fgrad_t + term
    fgrad_ref[...] = fgrad_t.T.astype(BF16)
    store(1, fgrad_ref, fgrad_hbm)
    for k in range(1, n_row):
        wait_row(sum_at + 1, w_all, k)
    for k in range(n_row):
        wgrad_ref[k * chunk:(k + 1) * chunk, :] = w_all[k, :chunk, :]
    store(2, wgrad_ref, wgrad_hbm)
    for copy in sent:
        copy.wait_send()
    for copy in stores:
        copy.wait()


def finish_kernel(count, *refs):
    sem = refs[-1]
    copies = [
        pltpu.make_async_copy(refs[n], refs[count + n], sem.at[n]) for n in range(count)
    ]
    for copy in copies:
        copy.start()
    for copy in copies:
        copy.wait()


def shards(
    n_row, n_col,
    features, weight, bias, node_scale, cotangent, tile_row, tile_col, tile_count, tile_values
):
    width = features.shape[1]
    slots = tile_row.shape[-1]
    assert features.shape[0] == BLOCK
    chunk = width // n_row
    halves = 2
    part = width // halves
    hbm = pl.BlockSpec(memory_space=pltpu.HBM)
    peers = n_row + n_col
    shapes = (
        jax.ShapeDtypeStruct((BLOCK, width), BF16),
        jax.ShapeDtypeStruct((BLOCK, width), BF16),
        jax.ShapeDtypeStruct((width, width), F32),
        jax.ShapeDtypeStruct((1, width), F32),
    )
    results = pl.pallas_call(
        functools.partial(layer_kernel, n_row, n_col, slots, halves),
        out_shape=shapes,
        in_specs=[hbm] * 9,
        out_specs=(hbm,) * 4,
        scratch_shapes=[pltpu.VMEM(shape.shape, shape.dtype) for shape in shapes]
        + [
            pltpu.SemaphoreType.DMA((4,)),
            pltpu.SMEM((slots,), jnp.int32),
            pltpu.SMEM((slots,), jnp.int32),
            pltpu.SMEM((1,), jnp.int32),
            pltpu.VMEM((BLOCK, width), BF16),
            pltpu.VMEM((width, width), BF16),
            pltpu.VMEM((1, width), F32),
            pltpu.VMEM((1, BLOCK), F32),
            pltpu.VMEM((BLOCK, width), BF16),
            pltpu.VMEM((slots, BLOCK, BLOCK), BF16),
            pltpu.VMEM((slots, BLOCK, BLOCK), BF16),
            pltpu.VMEM((slots, part, BLOCK), F32),
            pltpu.VMEM((2 * halves, n_col, part, BLOCK), BF16),
            pltpu.VMEM((2 * halves, n_row, part, BLOCK), BF16),
            pltpu.VMEM((2 * halves, n_col, part, BLOCK), BF16),
            pltpu.VMEM((2 * halves, n_row, part, BLOCK), BF16),
            pltpu.VMEM((n_row, chunk + 8, width), F32),
            pltpu.VMEM((n_row, chunk + 8, width), F32),
            pltpu.VMEM((n_col, chunk + 8, width), F32),
            pltpu.VMEM((n_row, chunk + 8, width), F32),
            pltpu.SemaphoreType.DMA((9,)),
            pltpu.SemaphoreType.DMA((4 * halves + 2, peers)),
            pltpu.SemaphoreType.DMA((4 * halves + 2, peers)),
        ]
        + [pltpu.VMEM((n_col, part, BLOCK), BF16)] * (2 * halves)
        + [pltpu.VMEM((n_row, part, BLOCK), BF16)] * (2 * halves),
        compiler_params=pltpu.CompilerParams(
            collective_id=0, has_side_effects=True, vmem_limit_bytes=VMEM_LIMIT
        ),
    )(
        tile_row.reshape(slots), tile_col.reshape(slots), tile_count.reshape(1),
        features, weight, bias.reshape(1, width), node_scale.reshape(1, BLOCK), cotangent,
        tile_values.reshape(slots, BLOCK, BLOCK),
    )
    act, fgrad, wgrad, bgrad = pl.pallas_call(
        functools.partial(finish_kernel, 4),
        out_shape=shapes,
        in_specs=[pl.BlockSpec(memory_space=pl.ANY)] * 4,
        out_specs=(hbm,) * 4,
        scratch_shapes=[pltpu.SemaphoreType.DMA((4,))],
        compiler_params=pltpu.CompilerParams(vmem_limit_bytes=VMEM_LIMIT),
    )(*results)
    return act, fgrad, wgrad, bgrad.reshape(width)


def solution(mesh):
    placed = (
        P(("row", "col"), None),
        P(),
        P(),
        P(("row", "col")),
        P(("row", "col"), None),
        P("row", "col", None),
        P("row", "col", None),
        P("row", "col"),
        P("row", "col", None, None, None),
    )
    return jax.shard_map(
        functools.partial(shards, mesh.shape["row"], mesh.shape["col"]),
        mesh=mesh,
        in_specs=placed,
        out_specs=(P(("row", "col"), None), P(("row", "col"), None), P(), P()),
        check_vma=False,
    )
```

```python
import functools

import jax
import jax.numpy as jnp
from jax import lax
from jax.experimental import pallas as pl
from jax.experimental.pallas import tpu as pltpu
from jax.sharding import PartitionSpec as P

BLOCK = 256
VMEM_LIMIT = 60 * 1024 * 1024
MESH = pl.DeviceIdType.MESH
F32 = jnp.float32
BF16 = jnp.bfloat16


def dot(a, b, dims=((1,), (0,))):
    return lax.dot_general(a, b, (dims, ((), ())), preferred_element_type=F32)


def layer_kernel(
    n_row, n_col, slots, halves,
    rows_hbm, cols_hbm, count_hbm, features_hbm, weight_hbm, bias_hbm, scale_hbm, cotangent_hbm,
    tiles_hbm,
    act_hbm, fgrad_hbm, wgrad_hbm, bgrad_hbm,
    act_ref, fgrad_ref, wgrad_ref, bgrad_ref, store_sem, rows_ref, cols_ref, count_ref, features, weight, bias, scale_ref, cotangent,
    tiles, tiles_t, terms, out_row, out_col, in_row, in_col, pair,
    w_part, w_in, w_cross, w_all, load_sem, send_sem, recv_sem, *blocks,
):
    r = lax.axis_index("row")
    c = lax.axis_index("col")
    width = features.shape[1]
    chunk = width // n_row
    part = width // halves

    pairs = (
        (features_hbm, features), (scale_hbm, scale_ref), (rows_hbm, rows_ref), (cols_hbm, cols_ref),
        (count_hbm, count_ref), (tiles_hbm, tiles), (weight_hbm, weight), (bias_hbm, bias),
        (cotangent_hbm, cotangent),
    )
    loads = [pltpu.make_async_copy(src, dst, load_sem.at[n]) for n, (src, dst) in enumerate(pairs)]
    for load in loads:
        load.start()

    row_peers = [lax.rem(r + k, n_row) for k in range(n_row)]
    col_peers = [lax.rem(c + k, n_col) for k in range(n_col)]
    chips = n_row // 2
    sibling = r + 1 - 2 * lax.rem(r, 2)
    mates = [lax.rem(r + 2 * k, n_row) for k in range(chips)]
    mate_siblings = [lax.rem(sibling + 2 * k, n_row) for k in range(chips)]
    line = n_col == 4
    near = c + 1 - 2 * lax.rem(c, 2)
    cross = 2 - c // 2
    far = 3 * (1 - c // 2)
    middle = lax.rem((c + 1) // 2, 2)

    barrier = pltpu.get_barrier_semaphore()
    for peer in row_peers[1:]:
        pl.semaphore_signal(barrier, inc=1, device_id=(peer, c), device_id_type=MESH)
    for peer in col_peers[1:]:
        pl.semaphore_signal(barrier, inc=1, device_id=(r, peer), device_id_type=MESH)

    sent = []
    sent_by_middle = []
    sent_by_ends = []
    stores = []

    def store(n, src, dst):
        copy = pltpu.make_async_copy(src, dst, store_sem.at[n])
        copy.start()
        stores.append(copy)

    def to_row(stage, n, peer, src, dst, slot):
        copy = pltpu.make_async_remote_copy(
            src_ref=src, dst_ref=dst.at[slot],
            send_sem=send_sem.at[stage, n], recv_sem=recv_sem.at[stage, slot],
            device_id=(peer, c), device_id_type=MESH)
        copy.start()
        sent.append(copy)

    def to_col(stage, n, peer, src, dst, slot, when=None):
        copy = pltpu.make_async_remote_copy(
            src_ref=src, dst_ref=dst.at[slot],
            send_sem=send_sem.at[stage, n_row + n], recv_sem=recv_sem.at[stage, n_row + slot],
            device_id=(r, peer), device_id_type=MESH)
        if when is None:
            copy.start()
            sent.append(copy)
        else:
            pl.when(when)(copy.start)
            sent_by_middle.append(copy)

    def wait_row(stage, dst, slot):
        pltpu.make_async_remote_copy(
            src_ref=dst.at[slot], dst_ref=dst.at[slot],
            send_sem=send_sem.at[stage, 0], recv_sem=recv_sem.at[stage, slot],
            device_id=(sibling, c), device_id_type=MESH).wait_recv()

    def wait_col(stage, dst, slot):
        pltpu.make_async_remote_copy(
            src_ref=dst.at[slot], dst_ref=dst.at[slot],
            send_sem=send_sem.at[stage, 0], recv_sem=recv_sem.at[stage, n_row + slot],
            device_id=(sibling, c), device_id_type=MESH).wait_recv()

    x_row = blocks[: 2 * halves]
    x_col = blocks[2 * halves:]
    spread_at = 2 * halves
    pair_at = 4 * halves
    sum_at = 6 * halves

    def gather(step, block):
        xr, xc = x_row[step], x_col[step]
        xr[c] = block
        xc[r] = block
        if step == 0:
            pl.semaphore_wait(barrier, n_row + n_col - 2)
        if line:
            to_col(step, 0, cross, xr.at[c], xr, c)
            to_col(step, 1, near, xr.at[c], xr, c)
            to_col(step, 2, far, xr.at[c], xr, c, when=middle == 1)
        else:
            for k in range(1, n_col):
                to_col(step, k, col_peers[k], xr.at[c], xr, c)
        for k in range(1, chips):
            to_row(step, k, mates[k], xc.at[r], xc, r)
        to_row(step, chips, sibling, xc.at[r], xc, r)

    def forward(step):
        xr, xc = x_row[step], x_col[step]
        for k in range(1, chips):
            wait_row(step, xc, mates[k])
            to_row(step, chips + k, sibling, xc.at[mates[k]], xc, mates[k])
        if line:
            @pl.when(middle == 1)
            def _():
                wait_col(step, xr, far)
            to_col(step, 3, near, xr.at[far], xr, far, when=middle == 1)

    def partial(at, index, weights):
        total = None
        for t in range(slots):
            term = terms[t] * jnp.where(at[t] == index, weights[t], 0.0)
            total = term if total is None else total + term
        return total

    def spread(step, row_at, col_at, weights):
        xr, xc = x_row[step], x_col[step]
        row_out, col_out, row_in, col_in = (
            ref.at[step] for ref in (out_row, out_col, in_row, in_col))
        stage = spread_at + step
        wait_row(step, xc, sibling)
        for k in range(1, chips):
            wait_row(step, xc, mate_siblings[k])
        for t in range(slots):
            terms[t] = dot(xc[col_at[t]], tiles_t[t])
        if line:
            relayed = pltpu.make_async_remote_copy(
                src_ref=row_out.at[2], dst_ref=row_in.at[n_col],
                send_sem=send_sem.at[stage, n_row + 2], recv_sem=recv_sem.at[stage, n_row + n_col],
                device_id=(r, near), device_id_type=MESH)

            @pl.when(middle == 0)
            def _():
                row_out[2] = partial(row_at, far, weights).astype(BF16)
                row_in[far] = jnp.zeros_like(row_in[far])
                relayed.start()
            sent_by_ends.append(relayed)
            row_out[0] = partial(row_at, cross, weights).astype(BF16)
            to_col(stage, 0, cross, row_out.at[0], row_in, c)
            row_out[1] = partial(row_at, near, weights).astype(BF16)
            to_col(stage, 1, near, row_out.at[1], row_in, c)
            row_in[c] = partial(row_at, c, weights).astype(BF16)

            @pl.when(middle == 1)
            def _():
                wait_col(stage, row_in, n_col)
                row_out[2] = (partial(row_at, far, weights) + row_in[n_col].astype(F32)).astype(BF16)
            to_col(stage, 2, far, row_out.at[2], row_in, c, when=middle == 1)
        else:
            for k in range(1, n_col):
                row_out[k - 1] = partial(row_at, col_peers[k], weights).astype(BF16)
                to_col(stage, k, col_peers[k], row_out.at[k - 1], row_in, c)
            row_in[c] = partial(row_at, c, weights).astype(BF16)

        if line:
            wait_col(step, xr, near)
            wait_col(step, xr, cross)

            @pl.when(middle == 0)
            def _():
                wait_col(step, xr, far)
        else:
            for k in range(1, n_col):
                wait_col(step, xr, col_peers[k])
        for t in range(slots):
            terms[t] = dot(xr[row_at[t]], tiles[t])
        for k in range(1, chips):
            col_out[k] = partial(col_at, mate_siblings[k], weights).astype(BF16)
            to_row(pair_at + step, k, sibling, col_out.at[k], pair.at[step], k)
        col_out[0] = partial(col_at, sibling, weights).astype(BF16)
        to_row(stage, 0, sibling, col_out.at[0], col_in, chips)
        col_in[0] = partial(col_at, r, weights).astype(BF16)
        for k in range(1, chips):
            mine = partial(col_at, mates[k], weights)
            wait_row(pair_at + step, pair.at[step], k)
            col_out[chips + k] = (mine + pair[step, k].astype(F32)).astype(BF16)
            to_row(stage, k, mates[k], col_out.at[chips + k], col_in, k)

    def collect(step, own):
        row_in, col_in = in_row.at[step], in_col.at[step]
        stage = spread_at + step
        if line:
            wait_col(stage, row_in, near)
            wait_col(stage, row_in, cross)

            @pl.when(middle == 1)
            def _():
                wait_col(stage, row_in, far)
        else:
            for k in range(1, n_col):
                wait_col(stage, row_in, col_peers[k])
        total = own.astype(F32)
        for k in range(n_col):
            total = total + row_in[k].astype(F32)
        for k in range(1, chips + 1):
            wait_row(stage, col_in, k)
        for k in range(chips + 1):
            total = total + col_in[k].astype(F32)
        return total

    for load in loads[:2]:
        load.wait()
    scale = scale_ref[...]
    scaled = (scale * features[...].astype(F32).T).astype(BF16)
    for h in range(halves):
        gather(h, scaled[h * part:(h + 1) * part])
    for load in loads[2:]:
        load.wait()
    row_at = [rows_ref[t] for t in range(slots)]
    col_at = [cols_ref[t] for t in range(slots)]
    count = count_ref[0]
    weights = [
        jnp.where(
            t < count,
            jnp.where(r * n_col + row_at[t] == col_at[t] * n_col + c, 0.5, 1.0),
            0.0,
        ).astype(F32)
        for t in range(slots)
    ]
    for t in range(slots):
        tiles_t[t] = tiles[t].T
    for h in range(halves):
        forward(h)
        spread(h, row_at, col_at, weights)
    mixed = jnp.concatenate(
        [collect(h, scaled[h * part:(h + 1) * part]) for h in range(halves)], axis=0)
    high = mixed.astype(BF16)
    low = (mixed - high.astype(F32)).astype(BF16)
    weight_t = weight[...].T
    bias_t = jnp.broadcast_to(bias[...], (BLOCK, width)).T
    cotangent_t = cotangent[...].astype(F32).T
    acts, deltas, scaled_deltas = [], [], []
    for h in range(halves):
        rows = slice(h * part, (h + 1) * part)
        product = dot(weight_t[rows], high) + dot(weight_t[rows], low)
        preact = scale * product + bias_t[rows]
        sig = 1.0 / (1.0 + jnp.exp(-preact))
        delta = cotangent_t[rows] * sig * (1.0 + preact * (1.0 - sig))
        scaled_delta = (scale * delta).astype(BF16)
        gather(halves + h, scaled_delta)
        acts.append(preact * sig)
        deltas.append(delta)
        scaled_deltas.append(scaled_delta)

    local = dot(high, jnp.concatenate(scaled_deltas, axis=0), ((1,), (1,)))
    local_bias = jnp.sum(jnp.concatenate(deltas, axis=0).T, axis=0, keepdims=True)
    for k in range(n_row):
        w_part[k, :chunk, :] = local[k * chunk:(k + 1) * chunk]
        w_part[k, chunk:, :] = jnp.broadcast_to(local_bias, (8, width))
    for k in range(1, n_row):
        to_row(sum_at, k, row_peers[k], w_part.at[row_peers[k]], w_in, r)
    w_in[r] = w_part[r]
    act_ref[...] = jnp.concatenate(acts, axis=0).T.astype(BF16)
    store(0, act_ref, act_hbm)
    for h in range(halves - 1):
        forward(halves + h)
        spread(halves + h, row_at, col_at, weights)
    for k in range(1, n_row):
        wait_row(sum_at, w_in, row_peers[k])
    summed = w_in[0]
    for k in range(1, n_row):
        summed = summed + w_in[k]
    w_cross[c] = summed
    for k in range(1, n_col):
        to_col(sum_at, k, col_peers[k], w_cross.at[c], w_cross, c)
    forward(2 * halves - 1)
    spread(2 * halves - 1, row_at, col_at, weights)
    for k in range(1, n_col):
        wait_col(sum_at, w_cross, col_peers[k])
    summed = w_cross[0]
    for k in range(1, n_col):
        summed = summed + w_cross[k]
    w_all[r] = summed
    for k in range(1, n_row):
        to_row(sum_at + 1, k, row_peers[k], w_all.at[r], w_all, r)
    bgrad_ref[...] = summed[chunk:chunk + 1]
    store(3, bgrad_ref, bgrad_hbm)

    fgrad_t = None
    for h in range(halves):
        proj_grad = (scale * collect(halves + h, scaled_deltas[h])).astype(BF16)
        term = dot(weight[:, h * part:(h + 1) * part], proj_grad)
        fgrad_t = term if fgrad_t is None else fgrad_t + term
    fgrad_ref[...] = fgrad_t.T.astype(BF16)
    store(1, fgrad_ref, fgrad_hbm)
    for k in range(1, n_row):
        wait_row(sum_at + 1, w_all, row_peers[k])
    for k in range(n_row):
        wgrad_ref[k * chunk:(k + 1) * chunk, :] = w_all[k, :chunk, :]
    store(2, wgrad_ref, wgrad_hbm)
    for copy in sent:
        copy.wait_send()

    @pl.when(middle == 1)
    def _():
        for copy in sent_by_middle:
            copy.wait_send()

    @pl.when(middle == 0)
    def _():
        for copy in sent_by_ends:
            copy.wait_send()
    for copy in stores:
        copy.wait()


def finish_kernel(count, *refs):
    sources, results, held = (refs[n * count:(n + 1) * count] for n in range(3))
    sem = refs[-1]
    fetches = [pltpu.make_async_copy(sources[n], held[n], sem.at[0, n]) for n in range(count)]
    stores = [pltpu.make_async_copy(held[n], results[n], sem.at[1, n]) for n in range(count)]
    for fetch in fetches:
        fetch.start()
    for n in range(count):
        fetches[n].wait()
        stores[n].start()
    for copy in stores:
        copy.wait()


def shards(
    n_row, n_col,
    features, weight, bias, node_scale, cotangent, tile_row, tile_col, tile_count, tile_values
):
    width = features.shape[1]
    slots = tile_row.shape[-1]
    assert features.shape[0] == BLOCK
    chunk = width // n_row
    halves = 2
    part = width // halves
    hbm = pl.BlockSpec(memory_space=pltpu.HBM)
    peers = n_row + n_col
    shapes = (
        jax.ShapeDtypeStruct((BLOCK, width), BF16),
        jax.ShapeDtypeStruct((BLOCK, width), BF16),
        jax.ShapeDtypeStruct((width, width), F32),
        jax.ShapeDtypeStruct((1, width), F32),
    )
    results = pl.pallas_call(
        functools.partial(layer_kernel, n_row, n_col, slots, halves),
        out_shape=shapes,
        in_specs=[hbm] * 9,
        out_specs=(hbm,) * 4,
        scratch_shapes=[pltpu.VMEM(shape.shape, shape.dtype) for shape in shapes]
        + [
            pltpu.SemaphoreType.DMA((4,)),
            pltpu.SMEM((slots,), jnp.int32),
            pltpu.SMEM((slots,), jnp.int32),
            pltpu.SMEM((1,), jnp.int32),
            pltpu.VMEM((BLOCK, width), BF16),
            pltpu.VMEM((width, width), BF16),
            pltpu.VMEM((1, width), F32),
            pltpu.VMEM((1, BLOCK), F32),
            pltpu.VMEM((BLOCK, width), BF16),
            pltpu.VMEM((slots, BLOCK, BLOCK), BF16),
            pltpu.VMEM((slots, BLOCK, BLOCK), BF16),
            pltpu.VMEM((slots, part, BLOCK), F32),
            pltpu.VMEM((2 * halves, n_col, part, BLOCK), BF16),
            pltpu.VMEM((2 * halves, n_row, part, BLOCK), BF16),
            pltpu.VMEM((2 * halves, n_col + 1, part, BLOCK), BF16),
            pltpu.VMEM((2 * halves, n_row // 2 + 1, part, BLOCK), BF16),
            pltpu.VMEM((2 * halves, n_row // 2, part, BLOCK), BF16),
            pltpu.VMEM((n_row, chunk + 8, width), F32),
            pltpu.VMEM((n_row, chunk + 8, width), F32),
            pltpu.VMEM((n_col, chunk + 8, width), F32),
            pltpu.VMEM((n_row, chunk + 8, width), F32),
            pltpu.SemaphoreType.DMA((9,)),
            pltpu.SemaphoreType.DMA((6 * halves + 2, peers + 1)),
            pltpu.SemaphoreType.DMA((6 * halves + 2, peers + 1)),
        ]
        + [pltpu.VMEM((n_col, part, BLOCK), BF16)] * (2 * halves)
        + [pltpu.VMEM((n_row, part, BLOCK), BF16)] * (2 * halves),
        compiler_params=pltpu.CompilerParams(
            collective_id=0, has_side_effects=True, vmem_limit_bytes=VMEM_LIMIT
        ),
    )(
        tile_row.reshape(slots), tile_col.reshape(slots), tile_count.reshape(1),
        features, weight, bias.reshape(1, width), node_scale.reshape(1, BLOCK), cotangent,
        tile_values.reshape(slots, BLOCK, BLOCK),
    )
    act, fgrad, wgrad, bgrad = pl.pallas_call(
        functools.partial(finish_kernel, 4),
        out_shape=shapes,
        in_specs=[pl.BlockSpec(memory_space=pl.ANY)] * 4,
        out_specs=(hbm,) * 4,
        scratch_shapes=[pltpu.VMEM(shape.shape, shape.dtype) for shape in shapes]
        + [pltpu.SemaphoreType.DMA((2, 4))],
        compiler_params=pltpu.CompilerParams(vmem_limit_bytes=VMEM_LIMIT),
    )(*results)
    return act, fgrad, wgrad, bgrad.reshape(width)


def solution(mesh):
    placed = (
        P(("row", "col"), None),
        P(),
        P(),
        P(("row", "col")),
        P(("row", "col"), None),
        P("row", "col", None),
        P("row", "col", None),
        P("row", "col"),
        P("row", "col", None, None, None),
    )
    return jax.shard_map(
        functools.partial(shards, mesh.shape["row"], mesh.shape["col"]),
        mesh=mesh,
        in_specs=placed,
        out_specs=(P(("row", "col"), None), P(("row", "col"), None), P(), P()),
        check_vma=False,
    )
```

```python
import functools

import jax
import jax.numpy as jnp
from jax import lax
from jax.experimental import pallas as pl
from jax.experimental.pallas import tpu as pltpu
from jax.sharding import PartitionSpec as P

BLOCK = 256
VMEM_LIMIT = 60 * 1024 * 1024
MESH = pl.DeviceIdType.MESH
F32 = jnp.float32
BF16 = jnp.bfloat16


def dot(a, b, dims=((1,), (0,))):
    return lax.dot_general(a, b, (dims, ((), ())), preferred_element_type=F32)


def layer_kernel(
    n_row, n_col, slots,
    rows_hbm, cols_hbm, count_hbm, features_hbm, weight_hbm, bias_hbm, scale_hbm, cotangent_hbm,
    tiles_hbm,
    act_hbm, fgrad_hbm, wgrad_hbm, bgrad_hbm,
    act_ref, fgrad_ref, wgrad_ref, bgrad_ref, store_sem, rows_ref, cols_ref, count_ref,
    features, weight, bias, scale_ref, cotangent,
    tiles, tiles_t, terms, out_row, out_col, in_row, in_col,
    w_part, w_in, w_cross, w_all, load_sem, send_row_sem, send_col_sem, recv_row_sem, recv_col_sem,
    x_row0, x_row1, x_col0, x_col1,
):
    r = lax.axis_index("row")
    c = lax.axis_index("col")
    width = features.shape[1]
    chunk = width // n_row

    pairs = (
        (features_hbm, features), (scale_hbm, scale_ref), (rows_hbm, rows_ref), (cols_hbm, cols_ref),
        (count_hbm, count_ref), (tiles_hbm, tiles), (weight_hbm, weight), (bias_hbm, bias),
        (cotangent_hbm, cotangent),
    )
    loads = [pltpu.make_async_copy(src, dst, load_sem.at[n]) for n, (src, dst) in enumerate(pairs)]
    for load in loads:
        load.start()

    def row_peer(k):
        return lax.rem(r + k, n_row)

    def col_peer(k):
        return lax.rem(c + k, n_col)

    def each(first, last, body):
        def step(k, carry):
            body(k)
            return carry
        lax.fori_loop(first, last, step, 0)

    barrier = pltpu.get_barrier_semaphore()
    each(1, n_row, lambda k: pl.semaphore_signal(
        barrier, inc=1, device_id=(row_peer(k), c), device_id_type=MESH))
    each(1, n_col, lambda k: pl.semaphore_signal(
        barrier, inc=1, device_id=(r, col_peer(k)), device_id_type=MESH))

    def row_copy(stage, k, src, dst):
        return pltpu.make_async_remote_copy(
            src_ref=src, dst_ref=dst, send_sem=send_row_sem.at[stage], recv_sem=recv_row_sem.at[stage],
            device_id=(row_peer(k), c), device_id_type=MESH)

    def col_copy(stage, k, src, dst):
        return pltpu.make_async_remote_copy(
            src_ref=src, dst_ref=dst, send_sem=send_col_sem.at[stage], recv_sem=recv_col_sem.at[stage],
            device_id=(r, col_peer(k)), device_id_type=MESH)

    def row_all(stage, buffer):
        whole = buffer.at[pl.ds(0, n_row - 1)]
        return row_copy(stage, 1, whole, whole)

    def col_all(stage, buffer):
        whole = buffer.at[pl.ds(0, n_col - 1)]
        return col_copy(stage, 1, whole, whole)

    x_row = (x_row0, x_row1)
    x_col = (x_col0, x_col1)

    def store(n, src, dst):
        copy = pltpu.make_async_copy(src, dst, store_sem.at[n])
        copy.start()
        stores.append(copy)

    stores = []

    def gather(phase, block):
        xr, xc = x_row[phase], x_col[phase]
        xr[c] = block
        xc[r] = block
        if phase == 0:
            pl.semaphore_wait(barrier, n_row + n_col - 2)
        each(1, n_col, lambda k: col_copy(phase, k, xr.at[c], xr.at[c]).start())
        each(1, n_row, lambda k: row_copy(phase, k, xc.at[r], xc.at[r]).start())

    def partial(at, index):
        total = None
        for t in range(slots):
            term = terms[t] * jnp.where(at[t] == index, weights[t], 0.0)
            total = term if total is None else total + term
        return total.astype(BF16)

    def spread(phase, between=None):
        xr, xc = x_row[phase], x_col[phase]
        stage = 2 + phase
        col_all(phase, xr).wait_recv()
        for t in range(slots):
            terms[t] = dot(xr[row_at[t]], tiles[t])

        def to_row(k):
            out_col[phase, k] = partial(col_at, row_peer(k))
            row_copy(stage, k, out_col.at[phase, k], in_col.at[phase, r]).start()

        each(1, n_row, to_row)
        in_col[phase, r] = partial(col_at, r)
        if between is not None:
            between()
        row_all(phase, xc).wait_recv()
        for t in range(slots):
            terms[t] = dot(xc[col_at[t]], tiles_t[t])

        def to_col(k):
            out_row[phase, k] = partial(row_at, col_peer(k))
            col_copy(stage, k, out_row.at[phase, k], in_row.at[phase, c]).start()

        each(1, n_col, to_col)
        in_row[phase, c] = partial(row_at, c)

    def collect(phase, own):
        total = own.astype(F32)
        row_all(2 + phase, in_col.at[phase]).wait_recv()
        for k in range(n_row):
            total = total + in_col[phase, k].astype(F32)
        col_all(2 + phase, in_row.at[phase]).wait_recv()
        for k in range(n_col):
            total = total + in_row[phase, k].astype(F32)
        return total

    for load in loads[:2]:
        load.wait()
    scale = scale_ref[...]
    scaled = (scale * features[...].astype(F32).T).astype(BF16)
    gather(0, scaled)
    for load in loads[2:]:
        load.wait()
    row_at = [rows_ref[t] for t in range(slots)]
    col_at = [cols_ref[t] for t in range(slots)]
    count = count_ref[0]
    weights = [
        jnp.where(
            t < count,
            jnp.where(r * n_col + row_at[t] == col_at[t] * n_col + c, 0.5, 1.0),
            0.0,
        ).astype(F32)
        for t in range(slots)
    ]

    def transpose(t):
        tiles_t[t] = tiles[t].T

    each(0, slots, transpose)
    spread(0)
    weight_t = weight[...].T
    bias_t = jnp.broadcast_to(bias[...], (BLOCK, width)).T
    cotangent_t = cotangent[...].astype(F32).T
    mixed = collect(0, scaled)
    high = mixed.astype(BF16)
    low = (mixed - high.astype(F32)).astype(BF16)
    product = dot(weight_t, high) + dot(weight_t, low)
    preact = scale * product + bias_t
    sig = 1.0 / (1.0 + jnp.exp(-preact))
    delta = cotangent_t * sig * (1.0 + preact * (1.0 - sig))
    scaled_delta = (scale * delta).astype(BF16)
    gather(1, scaled_delta)

    local = dot(high, scaled_delta, ((1,), (1,)))
    local_bias = jnp.sum(delta.T, axis=0, keepdims=True)
    for k in range(n_row):
        w_part[k, :chunk, :] = local[k * chunk:(k + 1) * chunk]
        w_part[k, chunk:, :] = jnp.broadcast_to(local_bias, (8, width))
    each(1, n_row, lambda k: row_copy(4, k, w_part.at[row_peer(k)], w_in.at[r]).start())
    w_in[r] = w_part[r]
    act_ref[...] = (preact * sig).T.astype(BF16)
    store(0, act_ref, act_hbm)

    def sum_over_row():
        row_all(4, w_in).wait_recv()
        summed = w_in[0]
        for k in range(1, n_row):
            summed = summed + w_in[k]
        w_cross[c] = summed
        each(1, n_col, lambda k: col_copy(4, k, w_cross.at[c], w_cross.at[c]).start())

    spread(1, sum_over_row)
    col_all(4, w_cross).wait_recv()
    summed = w_cross[0]
    for k in range(1, n_col):
        summed = summed + w_cross[k]
    w_all[r] = summed
    each(1, n_row, lambda k: row_copy(5, k, w_all.at[r], w_all.at[r]).start())
    bgrad_ref[...] = summed[chunk:chunk + 1]
    store(3, bgrad_ref, bgrad_hbm)

    proj_grad = (scale * collect(1, scaled_delta)).astype(BF16)
    fgrad_ref[...] = dot(weight[...], proj_grad).T.astype(BF16)
    store(1, fgrad_ref, fgrad_hbm)
    row_all(5, w_all).wait_recv()
    for k in range(n_row):
        wgrad_ref[k * chunk:(k + 1) * chunk, :] = w_all[k, :chunk, :]
    store(2, wgrad_ref, wgrad_hbm)
    for stage in range(6):
        row_all(stage, x_col0 if stage < 4 else w_in).wait_send()
    for stage in range(5):
        col_all(stage, x_row0 if stage < 4 else w_cross).wait_send()
    for copy in stores:
        copy.wait()


def finish_kernel(count, *refs):
    sources, results, held = (refs[n * count:(n + 1) * count] for n in range(3))
    sem = refs[-1]
    fetches = [pltpu.make_async_copy(sources[n], held[n], sem.at[0, n]) for n in range(count)]
    stores = [pltpu.make_async_copy(held[n], results[n], sem.at[1, n]) for n in range(count)]
    for fetch in fetches:
        fetch.start()
    for n in range(count):
        fetches[n].wait()
        stores[n].start()
    for copy in stores:
        copy.wait()


def shards(
    n_row, n_col,
    features, weight, bias, node_scale, cotangent, tile_row, tile_col, tile_count, tile_values
):
    width = features.shape[1]
    slots = tile_row.shape[-1]
    assert features.shape[0] == BLOCK
    chunk = width // n_row
    hbm = pl.BlockSpec(memory_space=pltpu.HBM)
    shapes = (
        jax.ShapeDtypeStruct((BLOCK, width), BF16),
        jax.ShapeDtypeStruct((BLOCK, width), BF16),
        jax.ShapeDtypeStruct((width, width), F32),
        jax.ShapeDtypeStruct((1, width), F32),
    )
    results = pl.pallas_call(
        functools.partial(layer_kernel, n_row, n_col, slots),
        out_shape=shapes,
        in_specs=[hbm] * 9,
        out_specs=(hbm,) * 4,
        scratch_shapes=[pltpu.VMEM(shape.shape, shape.dtype) for shape in shapes]
        + [
            pltpu.SemaphoreType.DMA((4,)),
            pltpu.SMEM((slots,), jnp.int32),
            pltpu.SMEM((slots,), jnp.int32),
            pltpu.SMEM((1,), jnp.int32),
            pltpu.VMEM((BLOCK, width), BF16),
            pltpu.VMEM((width, width), BF16),
            pltpu.VMEM((1, width), F32),
            pltpu.VMEM((1, BLOCK), F32),
            pltpu.VMEM((BLOCK, width), BF16),
            pltpu.VMEM((slots, BLOCK, BLOCK), BF16),
            pltpu.VMEM((slots, BLOCK, BLOCK), BF16),
            pltpu.VMEM((slots, width, BLOCK), F32),
            pltpu.VMEM((2, n_col, width, BLOCK), BF16),
            pltpu.VMEM((2, n_row, width, BLOCK), BF16),
            pltpu.VMEM((2, n_col, width, BLOCK), BF16),
            pltpu.VMEM((2, n_row, width, BLOCK), BF16),
            pltpu.VMEM((n_row, chunk + 8, width), F32),
            pltpu.VMEM((n_row, chunk + 8, width), F32),
            pltpu.VMEM((n_col, chunk + 8, width), F32),
            pltpu.VMEM((n_row, chunk + 8, width), F32),
            pltpu.SemaphoreType.DMA((9,)),
            pltpu.SemaphoreType.DMA((6,)),
            pltpu.SemaphoreType.DMA((5,)),
            pltpu.SemaphoreType.DMA((6,)),
            pltpu.SemaphoreType.DMA((5,)),
            pltpu.VMEM((n_col, width, BLOCK), BF16),
            pltpu.VMEM((n_col, width, BLOCK), BF16),
            pltpu.VMEM((n_row, width, BLOCK), BF16),
            pltpu.VMEM((n_row, width, BLOCK), BF16),
        ],
        compiler_params=pltpu.CompilerParams(
            collective_id=0, has_side_effects=True, vmem_limit_bytes=VMEM_LIMIT
        ),
    )(
        tile_row.reshape(slots), tile_col.reshape(slots), tile_count.reshape(1),
        features, weight, bias.reshape(1, width), node_scale.reshape(1, BLOCK), cotangent,
        tile_values.reshape(slots, BLOCK, BLOCK),
    )
    act, fgrad, wgrad, bgrad = pl.pallas_call(
        functools.partial(finish_kernel, 4),
        out_shape=shapes,
        in_specs=[pl.BlockSpec(memory_space=pl.ANY)] * 4,
        out_specs=(hbm,) * 4,
        scratch_shapes=[pltpu.VMEM(shape.shape, shape.dtype) for shape in shapes]
        + [pltpu.SemaphoreType.DMA((2, 4))],
        compiler_params=pltpu.CompilerParams(vmem_limit_bytes=VMEM_LIMIT),
    )(*results)
    return act, fgrad, wgrad, bgrad.reshape(width)


def solution(mesh):
    placed = (
        P(("row", "col"), None),
        P(),
        P(),
        P(("row", "col")),
        P(("row", "col"), None),
        P("row", "col", None),
        P("row", "col", None),
        P("row", "col"),
        P("row", "col", None, None, None),
    )
    return jax.shard_map(
        functools.partial(shards, mesh.shape["row"], mesh.shape["col"]),
        mesh=mesh,
        in_specs=placed,
        out_specs=(P(("row", "col"), None), P(("row", "col"), None), P(), P()),
        check_vma=False,
    )
```

```python
import functools

import jax
import jax.numpy as jnp
from jax import lax
from jax.experimental import pallas as pl
from jax.experimental.pallas import tpu as pltpu
from jax.sharding import PartitionSpec as P

BLOCK = 256
VMEM_LIMIT = 60 * 1024 * 1024
MESH = pl.DeviceIdType.MESH
F32 = jnp.float32
BF16 = jnp.bfloat16


def dot(a, b, dims=((1,), (0,))):
    return lax.dot_general(a, b, (dims, ((), ())), preferred_element_type=F32)


def layer_kernel(
    n_row, n_col, slots,
    rows_hbm, cols_hbm, count_hbm, features_hbm, weight_hbm, bias_hbm, scale_hbm, cotangent_hbm,
    tiles_hbm,
    act_hbm, fgrad_hbm, wgrad_hbm, bgrad_hbm,
    act_ref, fgrad_ref, wgrad_ref, bgrad_ref, store_sem, rows_ref, cols_ref, count_ref,
    features, weight, bias, scale_ref, cotangent,
    tiles, tiles_t, row_terms, col_terms, out_row, out_col, in_row, in_col,
    w_part, w_in, w_cross, w_all, load_sem, send_row_sem, send_col_sem, recv_row_sem, recv_col_sem,
    x_row0, x_row1, x_col0, x_col1,
):
    r = lax.axis_index("row")
    c = lax.axis_index("col")
    width = features.shape[1]
    chunk = width // n_row

    pairs = (
        (features_hbm, features), (scale_hbm, scale_ref), (rows_hbm, rows_ref), (cols_hbm, cols_ref),
        (count_hbm, count_ref), (tiles_hbm, tiles), (weight_hbm, weight), (bias_hbm, bias),
        (cotangent_hbm, cotangent),
    )
    loads = [pltpu.make_async_copy(src, dst, load_sem.at[n]) for n, (src, dst) in enumerate(pairs)]
    for load in loads:
        load.start()

    def row_peer(k):
        return lax.rem(r + k, n_row)

    def col_peer(k):
        return lax.rem(c + k, n_col)

    def each(first, last, body):
        def step(k, carry):
            body(k)
            return carry
        lax.fori_loop(first, last, step, 0)

    barrier = pltpu.get_barrier_semaphore()
    each(1, n_row, lambda k: pl.semaphore_signal(
        barrier, inc=1, device_id=(row_peer(k), c), device_id_type=MESH))
    each(1, n_col, lambda k: pl.semaphore_signal(
        barrier, inc=1, device_id=(r, col_peer(k)), device_id_type=MESH))

    def row_copy(stage, k, src, dst):
        return pltpu.make_async_remote_copy(
            src_ref=src, dst_ref=dst, send_sem=send_row_sem.at[stage], recv_sem=recv_row_sem.at[stage],
            device_id=(row_peer(k), c), device_id_type=MESH)

    def col_copy(stage, k, src, dst):
        return pltpu.make_async_remote_copy(
            src_ref=src, dst_ref=dst, send_sem=send_col_sem.at[stage], recv_sem=recv_col_sem.at[stage],
            device_id=(r, col_peer(k)), device_id_type=MESH)

    def row_all(stage, buffer):
        whole = buffer.at[pl.ds(0, n_row - 1)]
        return row_copy(stage, 1, whole, whole)

    def col_all(stage, buffer):
        whole = buffer.at[pl.ds(0, n_col - 1)]
        return col_copy(stage, 1, whole, whole)

    x_row = (x_row0, x_row1)
    x_col = (x_col0, x_col1)

    def store(n, src, dst):
        copy = pltpu.make_async_copy(src, dst, store_sem.at[n])
        copy.start()
        stores.append(copy)

    stores = []

    def gather(phase, block):
        xr, xc = x_row[phase], x_col[phase]
        xr[c] = block
        xc[r] = block
        if phase == 0:
            pl.semaphore_wait(barrier, n_row + n_col - 2)
        each(1, n_col, lambda k: col_copy(phase, k, xr.at[c], xr.at[c]).start())
        each(1, n_row, lambda k: row_copy(phase, k, xc.at[r], xc.at[r]).start())

    def partial(terms, at, index):
        total = None
        for t in range(slots):
            term = terms[t] * jnp.where(at[t] == index, weights[t], 0.0)
            total = term if total is None else total + term
        return total.astype(BF16)

    def spread(phase, between=None):
        xr, xc = x_row[phase], x_col[phase]
        stage = 2 + phase
        col_all(phase, xr).wait_recv()
        for t in range(slots):
            col_terms[t] = dot(xr[row_at[t]], tiles[t])
        row_all(phase, xc).wait_recv()
        for t in range(slots):
            row_terms[t] = dot(xc[col_at[t]], tiles_t[t])

        def to_col(k):
            out_row[phase, k] = partial(row_terms, row_at, col_peer(k))
            col_copy(stage, k, out_row.at[phase, k], in_row.at[phase, c]).start()

        def to_row(k):
            out_col[phase, k] = partial(col_terms, col_at, row_peer(k))
            row_copy(stage, k, out_col.at[phase, k], in_col.at[phase, r]).start()

        def to_both(k):
            to_col(k)
            to_row(k)

        common = min(n_row, n_col)
        each(1, common, to_both)
        each(common, n_col, to_col)
        each(common, n_row, to_row)
        in_row[phase, c] = partial(row_terms, row_at, c)
        in_col[phase, r] = partial(col_terms, col_at, r)
        if between is not None:
            between()

    def collect(phase, own):
        total = own.astype(F32)
        row_all(2 + phase, in_col.at[phase]).wait_recv()
        for k in range(n_row):
            total = total + in_col[phase, k].astype(F32)
        col_all(2 + phase, in_row.at[phase]).wait_recv()
        for k in range(n_col):
            total = total + in_row[phase, k].astype(F32)
        return total

    for load in loads[:2]:
        load.wait()
    scale = scale_ref[...]
    scaled = (scale * features[...].astype(F32).T).astype(BF16)
    gather(0, scaled)
    for load in loads[2:]:
        load.wait()
    row_at = [rows_ref[t] for t in range(slots)]
    col_at = [cols_ref[t] for t in range(slots)]
    count = count_ref[0]
    weights = [
        jnp.where(
            t < count,
            jnp.where(r * n_col + row_at[t] == col_at[t] * n_col + c, 0.5, 1.0),
            0.0,
        ).astype(F32)
        for t in range(slots)
    ]

    def transpose(t):
        tiles_t[t] = tiles[t].T

    each(0, slots, transpose)
    spread(0)
    weight_t = weight[...].T
    bias_t = jnp.broadcast_to(bias[...], (BLOCK, width)).T
    cotangent_t = cotangent[...].astype(F32).T
    mixed = collect(0, scaled)
    high = mixed.astype(BF16)
    low = (mixed - high.astype(F32)).astype(BF16)
    product = dot(weight_t, high) + dot(weight_t, low)
    preact = scale * product + bias_t
    sig = 1.0 / (1.0 + jnp.exp(-preact))
    delta = cotangent_t * sig * (1.0 + preact * (1.0 - sig))
    scaled_delta = (scale * delta).astype(BF16)
    gather(1, scaled_delta)

    local = dot(high, scaled_delta, ((1,), (1,)))
    local_bias = jnp.sum(delta.T, axis=0, keepdims=True)
    for k in range(n_row):
        w_part[k, :chunk, :] = local[k * chunk:(k + 1) * chunk]
        w_part[k, chunk:, :] = jnp.broadcast_to(local_bias, (8, width))
    each(1, n_row, lambda k: row_copy(4, k, w_part.at[row_peer(k)], w_in.at[r]).start())
    w_in[r] = w_part[r]
    act_ref[...] = (preact * sig).T.astype(BF16)
    store(0, act_ref, act_hbm)

    def sum_over_row():
        row_all(4, w_in).wait_recv()
        summed = w_in[0]
        for k in range(1, n_row):
            summed = summed + w_in[k]
        w_cross[c] = summed
        each(1, n_col, lambda k: col_copy(4, k, w_cross.at[c], w_cross.at[c]).start())

    spread(1, sum_over_row)
    col_all(4, w_cross).wait_recv()
    summed = w_cross[0]
    for k in range(1, n_col):
        summed = summed + w_cross[k]
    w_all[r] = summed
    each(1, n_row, lambda k: row_copy(5, k, w_all.at[r], w_all.at[r]).start())
    bgrad_ref[...] = summed[chunk:chunk + 1]
    store(3, bgrad_ref, bgrad_hbm)

    proj_grad = (scale * collect(1, scaled_delta)).astype(BF16)
    fgrad_ref[...] = dot(weight[...], proj_grad).T.astype(BF16)
    store(1, fgrad_ref, fgrad_hbm)
    row_all(5, w_all).wait_recv()
    for k in range(n_row):
        wgrad_ref[k * chunk:(k + 1) * chunk, :] = w_all[k, :chunk, :]
    store(2, wgrad_ref, wgrad_hbm)
    for stage in range(6):
        row_all(stage, x_col0 if stage < 4 else w_in).wait_send()
    for stage in range(5):
        col_all(stage, x_row0 if stage < 4 else w_cross).wait_send()
    for copy in stores:
        copy.wait()


def finish_kernel(count, *refs):
    sources, results, held = (refs[n * count:(n + 1) * count] for n in range(3))
    sem = refs[-1]
    fetches = [pltpu.make_async_copy(sources[n], held[n], sem.at[0, n]) for n in range(count)]
    stores = [pltpu.make_async_copy(held[n], results[n], sem.at[1, n]) for n in range(count)]
    for fetch in fetches:
        fetch.start()
    for n in range(count):
        fetches[n].wait()
        stores[n].start()
    for copy in stores:
        copy.wait()


def shards(
    n_row, n_col,
    features, weight, bias, node_scale, cotangent, tile_row, tile_col, tile_count, tile_values
):
    width = features.shape[1]
    slots = tile_row.shape[-1]
    assert features.shape[0] == BLOCK
    chunk = width // n_row
    hbm = pl.BlockSpec(memory_space=pltpu.HBM)
    shapes = (
        jax.ShapeDtypeStruct((BLOCK, width), BF16),
        jax.ShapeDtypeStruct((BLOCK, width), BF16),
        jax.ShapeDtypeStruct((width, width), F32),
        jax.ShapeDtypeStruct((1, width), F32),
    )
    results = pl.pallas_call(
        functools.partial(layer_kernel, n_row, n_col, slots),
        out_shape=shapes,
        in_specs=[hbm] * 9,
        out_specs=(hbm,) * 4,
        scratch_shapes=[pltpu.VMEM(shape.shape, shape.dtype) for shape in shapes]
        + [
            pltpu.SemaphoreType.DMA((4,)),
            pltpu.SMEM((slots,), jnp.int32),
            pltpu.SMEM((slots,), jnp.int32),
            pltpu.SMEM((1,), jnp.int32),
            pltpu.VMEM((BLOCK, width), BF16),
            pltpu.VMEM((width, width), BF16),
            pltpu.VMEM((1, width), F32),
            pltpu.VMEM((1, BLOCK), F32),
            pltpu.VMEM((BLOCK, width), BF16),
            pltpu.VMEM((slots, BLOCK, BLOCK), BF16),
            pltpu.VMEM((slots, BLOCK, BLOCK), BF16),
            pltpu.VMEM((slots, width, BLOCK), F32),
            pltpu.VMEM((slots, width, BLOCK), F32),
            pltpu.VMEM((2, n_col, width, BLOCK), BF16),
            pltpu.VMEM((2, n_row, width, BLOCK), BF16),
            pltpu.VMEM((2, n_col, width, BLOCK), BF16),
            pltpu.VMEM((2, n_row, width, BLOCK), BF16),
            pltpu.VMEM((n_row, chunk + 8, width), F32),
            pltpu.VMEM((n_row, chunk + 8, width), F32),
            pltpu.VMEM((n_col, chunk + 8, width), F32),
            pltpu.VMEM((n_row, chunk + 8, width), F32),
            pltpu.SemaphoreType.DMA((9,)),
            pltpu.SemaphoreType.DMA((6,)),
            pltpu.SemaphoreType.DMA((5,)),
            pltpu.SemaphoreType.DMA((6,)),
            pltpu.SemaphoreType.DMA((5,)),
            pltpu.VMEM((n_col, width, BLOCK), BF16),
            pltpu.VMEM((n_col, width, BLOCK), BF16),
            pltpu.VMEM((n_row, width, BLOCK), BF16),
            pltpu.VMEM((n_row, width, BLOCK), BF16),
        ],
        compiler_params=pltpu.CompilerParams(
            collective_id=0, has_side_effects=True, vmem_limit_bytes=VMEM_LIMIT
        ),
    )(
        tile_row.reshape(slots), tile_col.reshape(slots), tile_count.reshape(1),
        features, weight, bias.reshape(1, width), node_scale.reshape(1, BLOCK), cotangent,
        tile_values.reshape(slots, BLOCK, BLOCK),
    )
    act, fgrad, wgrad, bgrad = pl.pallas_call(
        functools.partial(finish_kernel, 4),
        out_shape=shapes,
        in_specs=[pl.BlockSpec(memory_space=pl.ANY)] * 4,
        out_specs=(hbm,) * 4,
        scratch_shapes=[pltpu.VMEM(shape.shape, shape.dtype) for shape in shapes]
        + [pltpu.SemaphoreType.DMA((2, 4))],
        compiler_params=pltpu.CompilerParams(vmem_limit_bytes=VMEM_LIMIT),
    )(*results)
    return act, fgrad, wgrad, bgrad.reshape(width)


def solution(mesh):
    placed = (
        P(("row", "col"), None),
        P(),
        P(),
        P(("row", "col")),
        P(("row", "col"), None),
        P("row", "col", None),
        P("row", "col", None),
        P("row", "col"),
        P("row", "col", None, None, None),
    )
    return jax.shard_map(
        functools.partial(shards, mesh.shape["row"], mesh.shape["col"]),
        mesh=mesh,
        in_specs=placed,
        out_specs=(P(("row", "col"), None), P(("row", "col"), None), P(), P()),
        check_vma=False,
    )
```

```python
import functools

import jax
import jax.numpy as jnp
from jax import lax
from jax.experimental import pallas as pl
from jax.experimental.pallas import tpu as pltpu
from jax.sharding import PartitionSpec as P

BLOCK = 256
VMEM_LIMIT = 60 * 1024 * 1024
MESH = pl.DeviceIdType.MESH
F32 = jnp.float32
BF16 = jnp.bfloat16


def dot(a, b, dims=((1,), (0,))):
    return lax.dot_general(a, b, (dims, ((), ())), preferred_element_type=F32)


def layer_kernel(
    n_row, n_col, slots,
    rows_hbm, cols_hbm, count_hbm, features_hbm, weight_hbm, bias_hbm, scale_hbm, cotangent_hbm,
    tiles_hbm,
    act_hbm, fgrad_hbm, wgrad_hbm, bgrad_hbm,
    act_ref, fgrad_ref, wgrad_ref, bgrad_ref, store_sem, rows_ref, cols_ref, count_ref,
    features, weight, bias, scale_ref, cotangent,
    tiles, tiles_t, row_terms, col_terms, out_row, out_col, in_row, in_col, pair,
    w_part, w_in, w_cross, w_all, load_sem, send_row_sem, send_col_sem, recv_row_sem, recv_col_sem,
    send_sib_sem, recv_sib_sem,
    x_row0, x_row1, x_col0, x_col1,
):
    r = lax.axis_index("row")
    c = lax.axis_index("col")
    width = features.shape[1]
    chunk = width // n_row

    pairs = (
        (features_hbm, features), (scale_hbm, scale_ref), (rows_hbm, rows_ref), (cols_hbm, cols_ref),
        (count_hbm, count_ref), (tiles_hbm, tiles), (weight_hbm, weight), (bias_hbm, bias),
        (cotangent_hbm, cotangent),
    )
    loads = [pltpu.make_async_copy(src, dst, load_sem.at[n]) for n, (src, dst) in enumerate(pairs)]
    for load in loads:
        load.start()

    def row_peer(k):
        return lax.rem(r + k, n_row)

    def col_peer(k):
        return lax.rem(c + k, n_col)

    chips = n_row // 2
    sibling = r + 1 - 2 * lax.rem(r, 2)

    def mate(k):
        return lax.rem(r + 2 * k, n_row)

    def mate_sibling(k):
        return lax.rem(sibling + 2 * k, n_row)

    def each(first, last, body):
        def step(k, carry):
            body(k)
            return carry
        lax.fori_loop(first, last, step, 0)

    barrier = pltpu.get_barrier_semaphore()
    each(1, n_row, lambda k: pl.semaphore_signal(
        barrier, inc=1, device_id=(row_peer(k), c), device_id_type=MESH))
    each(1, n_col, lambda k: pl.semaphore_signal(
        barrier, inc=1, device_id=(r, col_peer(k)), device_id_type=MESH))

    def row_copy(stage, k, src, dst):
        return pltpu.make_async_remote_copy(
            src_ref=src, dst_ref=dst, send_sem=send_row_sem.at[stage], recv_sem=recv_row_sem.at[stage],
            device_id=(row_peer(k), c), device_id_type=MESH)

    def col_copy(stage, k, src, dst):
        return pltpu.make_async_remote_copy(
            src_ref=src, dst_ref=dst, send_sem=send_col_sem.at[stage], recv_sem=recv_col_sem.at[stage],
            device_id=(r, col_peer(k)), device_id_type=MESH)

    def mate_copy(stage, k, src, dst):
        return pltpu.make_async_remote_copy(
            src_ref=src, dst_ref=dst, send_sem=send_row_sem.at[stage], recv_sem=recv_row_sem.at[stage],
            device_id=(mate(k), c), device_id_type=MESH)

    def sibling_copy(stage, src, dst):
        return pltpu.make_async_remote_copy(
            src_ref=src, dst_ref=dst, send_sem=send_sib_sem.at[stage], recv_sem=recv_sib_sem.at[stage],
            device_id=(sibling, c), device_id_type=MESH)

    def mate_all(stage, buffer):
        whole = buffer.at[pl.ds(0, chips - 1)]
        return mate_copy(stage, 1, whole, whole)

    def sibling_all(stage, buffer, count):
        whole = buffer.at[pl.ds(0, count)]
        return sibling_copy(stage, whole, whole)

    def row_all(stage, buffer):
        whole = buffer.at[pl.ds(0, n_row - 1)]
        return row_copy(stage, 1, whole, whole)

    def col_all(stage, buffer):
        whole = buffer.at[pl.ds(0, n_col - 1)]
        return col_copy(stage, 1, whole, whole)

    x_row = (x_row0, x_row1)
    x_col = (x_col0, x_col1)

    def store(n, src, dst):
        copy = pltpu.make_async_copy(src, dst, store_sem.at[n])
        copy.start()
        stores.append(copy)

    stores = []

    def gather(phase, block):
        xr, xc = x_row[phase], x_col[phase]
        xr[c] = block
        xc[r] = block
        if phase == 0:
            pl.semaphore_wait(barrier, n_row + n_col - 2)
        each(1, n_col, lambda k: col_copy(phase, k, xr.at[c], xr.at[c]).start())
        each(1, chips, lambda k: mate_copy(phase, k, xc.at[r], xc.at[r]).start())
        sibling_copy(phase, xc.at[r], xc.at[r]).start()

    def partial(terms, at, index, kind=BF16):
        total = None
        for t in range(slots):
            term = terms[t] * jnp.where(at[t] == index, weights[t], 0.0)
            total = term if total is None else total + term
        return total.astype(kind)

    def forward(phase):
        xc = x_col[phase]
        mate_all(phase, xc).wait_recv()
        each(1, chips, lambda k: sibling_copy(phase, xc.at[mate(k)], xc.at[mate(k)]).start())

    def spread(phase, between=None):
        xr, xc = x_row[phase], x_col[phase]
        stage = 2 + phase
        col_all(phase, xr).wait_recv()
        for t in range(slots):
            col_terms[t] = dot(xr[row_at[t]], tiles[t])

        def to_pair(k):
            out_col[phase, k] = partial(col_terms, col_at, mate_sibling(k))
            sibling_copy(stage, out_col.at[phase, k], pair.at[phase, k]).start()

        each(1, chips, to_pair)
        out_col[phase, 0] = partial(col_terms, col_at, sibling)
        sibling_copy(4 + phase, out_col.at[phase, 0], in_col.at[phase, chips]).start()
        sibling_all(phase, xc, chips).wait_recv()
        for t in range(slots):
            row_terms[t] = dot(xc[col_at[t]], tiles_t[t])

        def to_col(k):
            out_row[phase, k] = partial(row_terms, row_at, col_peer(k)).astype(BF16)
            col_copy(stage, k, out_row.at[phase, k], in_row.at[phase, c]).start()

        each(1, n_col, to_col)
        sibling_all(stage, pair.at[phase], chips - 1).wait_recv()

        def to_mate(k):
            mine = partial(col_terms, col_at, mate(k), F32) + pair[phase, k].astype(F32)
            out_col[phase, chips + k] = mine.astype(BF16)
            mate_copy(stage, k, out_col.at[phase, chips + k], in_col.at[phase, k]).start()

        each(1, chips, to_mate)
        in_col[phase, 0] = partial(col_terms, col_at, r)
        in_row[phase, c] = partial(row_terms, row_at, c)
        if between is not None:
            between()

    def collect(phase, own):
        total = own.astype(F32)
        sibling_all(4 + phase, in_col.at[phase], 1).wait_recv()
        mate_all(2 + phase, in_col.at[phase]).wait_recv()
        for k in range(chips + 1):
            total = total + in_col[phase, k].astype(F32)
        col_all(2 + phase, in_row.at[phase]).wait_recv()
        for k in range(n_col):
            total = total + in_row[phase, k].astype(F32)
        return total

    for load in loads[:2]:
        load.wait()
    scale = scale_ref[...]
    scaled = (scale * features[...].astype(F32).T).astype(BF16)
    gather(0, scaled)
    for load in loads[2:]:
        load.wait()
    row_at = [rows_ref[t] for t in range(slots)]
    col_at = [cols_ref[t] for t in range(slots)]
    count = count_ref[0]
    weights = [
        jnp.where(
            t < count,
            jnp.where(r * n_col + row_at[t] == col_at[t] * n_col + c, 0.5, 1.0),
            0.0,
        ).astype(F32)
        for t in range(slots)
    ]

    def transpose(t):
        tiles_t[t] = tiles[t].T

    each(0, slots, transpose)
    forward(0)
    spread(0)
    weight_t = weight[...].T
    bias_t = jnp.broadcast_to(bias[...], (BLOCK, width)).T
    cotangent_t = cotangent[...].astype(F32).T
    mixed = collect(0, scaled)
    high = mixed.astype(BF16)
    low = (mixed - high.astype(F32)).astype(BF16)
    product = dot(weight_t, high) + dot(weight_t, low)
    preact = scale * product + bias_t
    sig = 1.0 / (1.0 + jnp.exp(-preact))
    delta = cotangent_t * sig * (1.0 + preact * (1.0 - sig))
    scaled_delta = (scale * delta).astype(BF16)
    gather(1, scaled_delta)

    local = dot(high, scaled_delta, ((1,), (1,)))
    local_bias = jnp.sum(delta.T, axis=0, keepdims=True)
    for k in range(n_row):
        w_part[k, :chunk, :] = local[k * chunk:(k + 1) * chunk]
        w_part[k, chunk:, :] = jnp.broadcast_to(local_bias, (8, width))
    each(1, n_row, lambda k: row_copy(4, k, w_part.at[row_peer(k)], w_in.at[r]).start())
    w_in[r] = w_part[r]
    act_ref[...] = (preact * sig).T.astype(BF16)
    store(0, act_ref, act_hbm)

    def sum_over_row():
        row_all(4, w_in).wait_recv()
        summed = w_in[0]
        for k in range(1, n_row):
            summed = summed + w_in[k]
        w_cross[c] = summed
        each(1, n_col, lambda k: col_copy(4, k, w_cross.at[c], w_cross.at[c]).start())

    forward(1)
    spread(1, sum_over_row)
    col_all(4, w_cross).wait_recv()
    summed = w_cross[0]
    for k in range(1, n_col):
        summed = summed + w_cross[k]
    w_all[r] = summed
    each(1, n_row, lambda k: row_copy(5, k, w_all.at[r], w_all.at[r]).start())
    bgrad_ref[...] = summed[chunk:chunk + 1]
    store(3, bgrad_ref, bgrad_hbm)

    proj_grad = (scale * collect(1, scaled_delta)).astype(BF16)
    fgrad_ref[...] = dot(weight[...], proj_grad).T.astype(BF16)
    store(1, fgrad_ref, fgrad_hbm)
    row_all(5, w_all).wait_recv()
    for k in range(n_row):
        wgrad_ref[k * chunk:(k + 1) * chunk, :] = w_all[k, :chunk, :]
    store(2, wgrad_ref, wgrad_hbm)
    for stage in range(4):
        mate_all(stage, x_col0).wait_send()
    for stage in range(4, 6):
        row_all(stage, w_in).wait_send()
    for stage, count in enumerate((chips, chips, chips - 1, chips - 1, 1, 1)):
        sibling_all(stage, x_col0, count).wait_send()
    for stage in range(5):
        col_all(stage, x_row0 if stage < 4 else w_cross).wait_send()
    for copy in stores:
        copy.wait()


def finish_kernel(count, *refs):
    sources, results, held = (refs[n * count:(n + 1) * count] for n in range(3))
    sem = refs[-1]
    fetches = [pltpu.make_async_copy(sources[n], held[n], sem.at[0, n]) for n in range(count)]
    stores = [pltpu.make_async_copy(held[n], results[n], sem.at[1, n]) for n in range(count)]
    for fetch in fetches:
        fetch.start()
    for n in range(count):
        fetches[n].wait()
        stores[n].start()
    for copy in stores:
        copy.wait()


def shards(
    n_row, n_col,
    features, weight, bias, node_scale, cotangent, tile_row, tile_col, tile_count, tile_values
):
    width = features.shape[1]
    slots = tile_row.shape[-1]
    assert features.shape[0] == BLOCK
    chunk = width // n_row
    hbm = pl.BlockSpec(memory_space=pltpu.HBM)
    shapes = (
        jax.ShapeDtypeStruct((BLOCK, width), BF16),
        jax.ShapeDtypeStruct((BLOCK, width), BF16),
        jax.ShapeDtypeStruct((width, width), F32),
        jax.ShapeDtypeStruct((1, width), F32),
    )
    results = pl.pallas_call(
        functools.partial(layer_kernel, n_row, n_col, slots),
        out_shape=shapes,
        in_specs=[hbm] * 9,
        out_specs=(hbm,) * 4,
        scratch_shapes=[pltpu.VMEM(shape.shape, shape.dtype) for shape in shapes]
        + [
            pltpu.SemaphoreType.DMA((4,)),
            pltpu.SMEM((slots,), jnp.int32),
            pltpu.SMEM((slots,), jnp.int32),
            pltpu.SMEM((1,), jnp.int32),
            pltpu.VMEM((BLOCK, width), BF16),
            pltpu.VMEM((width, width), BF16),
            pltpu.VMEM((1, width), F32),
            pltpu.VMEM((1, BLOCK), F32),
            pltpu.VMEM((BLOCK, width), BF16),
            pltpu.VMEM((slots, BLOCK, BLOCK), BF16),
            pltpu.VMEM((slots, BLOCK, BLOCK), BF16),
            pltpu.VMEM((slots, width, BLOCK), F32),
            pltpu.VMEM((slots, width, BLOCK), F32),
            pltpu.VMEM((2, n_col, width, BLOCK), BF16),
            pltpu.VMEM((2, n_row, width, BLOCK), BF16),
            pltpu.VMEM((2, n_col, width, BLOCK), BF16),
            pltpu.VMEM((2, n_row // 2 + 1, width, BLOCK), BF16),
            pltpu.VMEM((2, n_row // 2, width, BLOCK), BF16),
            pltpu.VMEM((n_row, chunk + 8, width), F32),
            pltpu.VMEM((n_row, chunk + 8, width), F32),
            pltpu.VMEM((n_col, chunk + 8, width), F32),
            pltpu.VMEM((n_row, chunk + 8, width), F32),
            pltpu.SemaphoreType.DMA((9,)),
            pltpu.SemaphoreType.DMA((6,)),
            pltpu.SemaphoreType.DMA((5,)),
            pltpu.SemaphoreType.DMA((6,)),
            pltpu.SemaphoreType.DMA((5,)),
            pltpu.SemaphoreType.DMA((6,)),
            pltpu.SemaphoreType.DMA((6,)),
            pltpu.VMEM((n_col, width, BLOCK), BF16),
            pltpu.VMEM((n_col, width, BLOCK), BF16),
            pltpu.VMEM((n_row, width, BLOCK), BF16),
            pltpu.VMEM((n_row, width, BLOCK), BF16),
        ],
        compiler_params=pltpu.CompilerParams(
            collective_id=0, has_side_effects=True, vmem_limit_bytes=VMEM_LIMIT
        ),
    )(
        tile_row.reshape(slots), tile_col.reshape(slots), tile_count.reshape(1),
        features, weight, bias.reshape(1, width), node_scale.reshape(1, BLOCK), cotangent,
        tile_values.reshape(slots, BLOCK, BLOCK),
    )
    act, fgrad, wgrad, bgrad = pl.pallas_call(
        functools.partial(finish_kernel, 4),
        out_shape=shapes,
        in_specs=[pl.BlockSpec(memory_space=pl.ANY)] * 4,
        out_specs=(hbm,) * 4,
        scratch_shapes=[pltpu.VMEM(shape.shape, shape.dtype) for shape in shapes]
        + [pltpu.SemaphoreType.DMA((2, 4))],
        compiler_params=pltpu.CompilerParams(vmem_limit_bytes=VMEM_LIMIT),
    )(*results)
    return act, fgrad, wgrad, bgrad.reshape(width)


def solution(mesh):
    placed = (
        P(("row", "col"), None),
        P(),
        P(),
        P(("row", "col")),
        P(("row", "col"), None),
        P("row", "col", None),
        P("row", "col", None),
        P("row", "col"),
        P("row", "col", None, None, None),
    )
    return jax.shard_map(
        functools.partial(shards, mesh.shape["row"], mesh.shape["col"]),
        mesh=mesh,
        in_specs=placed,
        out_specs=(P(("row", "col"), None), P(("row", "col"), None), P(), P()),
        check_vma=False,
    )
```

```python
import functools

import jax
import jax.numpy as jnp
from jax import lax
from jax.experimental import pallas as pl
from jax.experimental.pallas import tpu as pltpu
from jax.sharding import PartitionSpec as P

BLOCK = 256
VMEM_LIMIT = 60 * 1024 * 1024
MESH = pl.DeviceIdType.MESH
F32 = jnp.float32
BF16 = jnp.bfloat16


def dot(a, b, dims=((1,), (0,))):
    return lax.dot_general(a, b, (dims, ((), ())), preferred_element_type=F32)


def layer_kernel(
    n_row, n_col, slots,
    rows_hbm, cols_hbm, count_hbm, features_hbm, weight_hbm, bias_hbm, scale_hbm, cotangent_hbm,
    tiles_hbm,
    act_hbm, fgrad_hbm, wgrad_hbm, bgrad_hbm,
    act_ref, fgrad_ref, wgrad_ref, bgrad_ref, store_sem, rows_ref, cols_ref, count_ref,
    features, weight, bias, scale_ref, cotangent,
    tiles, tiles_t, terms, out_row, out_col, in_row, in_col,
    w_part, w_in, w_cross, w_all, load_sem, send_row_sem, send_col_sem, recv_row_sem, recv_col_sem,
    send_sib_sem, recv_sib_sem,
    x_row0, x_row1, x_col0, x_col1,
):
    r = lax.axis_index("row")
    c = lax.axis_index("col")
    width = features.shape[1]
    chunk = width // n_row

    pairs = (
        (features_hbm, features), (scale_hbm, scale_ref), (rows_hbm, rows_ref), (cols_hbm, cols_ref),
        (count_hbm, count_ref), (tiles_hbm, tiles), (weight_hbm, weight), (bias_hbm, bias),
        (cotangent_hbm, cotangent),
    )
    loads = [pltpu.make_async_copy(src, dst, load_sem.at[n]) for n, (src, dst) in enumerate(pairs)]
    for load in loads:
        load.start()

    def row_peer(k):
        return lax.rem(r + k, n_row)

    def col_peer(k):
        return lax.rem(c + k, n_col)

    chips = n_row // 2
    sibling = r + 1 - 2 * lax.rem(r, 2)

    def mate(k):
        return lax.rem(r + 2 * k, n_row)

    def each(first, last, body):
        def step(k, carry):
            body(k)
            return carry
        lax.fori_loop(first, last, step, 0)

    barrier = pltpu.get_barrier_semaphore()
    each(1, n_row, lambda k: pl.semaphore_signal(
        barrier, inc=1, device_id=(row_peer(k), c), device_id_type=MESH))
    each(1, n_col, lambda k: pl.semaphore_signal(
        barrier, inc=1, device_id=(r, col_peer(k)), device_id_type=MESH))

    def row_copy(stage, k, src, dst):
        return pltpu.make_async_remote_copy(
            src_ref=src, dst_ref=dst, send_sem=send_row_sem.at[stage], recv_sem=recv_row_sem.at[stage],
            device_id=(row_peer(k), c), device_id_type=MESH)

    def col_copy(stage, k, src, dst):
        return pltpu.make_async_remote_copy(
            src_ref=src, dst_ref=dst, send_sem=send_col_sem.at[stage], recv_sem=recv_col_sem.at[stage],
            device_id=(r, col_peer(k)), device_id_type=MESH)

    def mate_copy(stage, k, src, dst):
        return pltpu.make_async_remote_copy(
            src_ref=src, dst_ref=dst, send_sem=send_row_sem.at[stage], recv_sem=recv_row_sem.at[stage],
            device_id=(mate(k), c), device_id_type=MESH)

    def sibling_copy(stage, src, dst):
        return pltpu.make_async_remote_copy(
            src_ref=src, dst_ref=dst, send_sem=send_sib_sem.at[stage], recv_sem=recv_sib_sem.at[stage],
            device_id=(sibling, c), device_id_type=MESH)

    def mate_all(stage, buffer):
        whole = buffer.at[pl.ds(0, chips - 1)]
        return mate_copy(stage, 1, whole, whole)

    def sibling_all(stage, buffer, count):
        whole = buffer.at[pl.ds(0, count)]
        return sibling_copy(stage, whole, whole)

    def row_all(stage, buffer):
        whole = buffer.at[pl.ds(0, n_row - 1)]
        return row_copy(stage, 1, whole, whole)

    def col_all(stage, buffer):
        whole = buffer.at[pl.ds(0, n_col - 1)]
        return col_copy(stage, 1, whole, whole)

    x_row = (x_row0, x_row1)
    x_col = (x_col0, x_col1)

    def store(n, src, dst):
        copy = pltpu.make_async_copy(src, dst, store_sem.at[n])
        copy.start()
        stores.append(copy)

    stores = []

    def gather(phase, block):
        xr, xc = x_row[phase], x_col[phase]
        xr[c] = block
        xc[r] = block
        if phase == 0:
            pl.semaphore_wait(barrier, n_row + n_col - 2)
        each(1, n_col, lambda k: col_copy(phase, k, xr.at[c], xr.at[c]).start())
        each(1, chips, lambda k: mate_copy(phase, k, xc.at[r], xc.at[r]).start())
        sibling_copy(phase, xc.at[r], xc.at[r]).start()

    def partial(at, index):
        total = None
        for t in range(slots):
            term = terms[t] * jnp.where(at[t] == index, weights[t], 0.0)
            total = term if total is None else total + term
        return total.astype(BF16)

    def forward(phase):
        xc = x_col[phase]
        mate_all(phase, xc).wait_recv()
        each(1, chips, lambda k: sibling_copy(phase, xc.at[mate(k)], xc.at[mate(k)]).start())

    def spread(phase, between=None):
        xr, xc = x_row[phase], x_col[phase]
        stage = 2 + phase
        col_all(phase, xr).wait_recv()
        for t in range(slots):
            terms[t] = dot(xr[row_at[t]], tiles[t])

        def to_row(k):
            out_col[phase, k] = partial(col_at, row_peer(k))
            row_copy(stage, k, out_col.at[phase, k], in_col.at[phase, r]).start()

        each(1, n_row, to_row)
        in_col[phase, r] = partial(col_at, r)
        if between is not None:
            between()
        sibling_all(phase, xc, chips).wait_recv()
        for t in range(slots):
            terms[t] = dot(xc[col_at[t]], tiles_t[t])

        def to_col(k):
            out_row[phase, k] = partial(row_at, col_peer(k))
            col_copy(stage, k, out_row.at[phase, k], in_row.at[phase, c]).start()

        each(1, n_col, to_col)
        in_row[phase, c] = partial(row_at, c)

    def collect(phase, own):
        total = own.astype(F32)
        row_all(2 + phase, in_col.at[phase]).wait_recv()
        for k in range(n_row):
            total = total + in_col[phase, k].astype(F32)
        col_all(2 + phase, in_row.at[phase]).wait_recv()
        for k in range(n_col):
            total = total + in_row[phase, k].astype(F32)
        return total

    for load in loads[:2]:
        load.wait()
    scale = scale_ref[...]
    scaled = (scale * features[...].astype(F32).T).astype(BF16)
    gather(0, scaled)
    for load in loads[2:]:
        load.wait()
    row_at = [rows_ref[t] for t in range(slots)]
    col_at = [cols_ref[t] for t in range(slots)]
    count = count_ref[0]
    weights = [
        jnp.where(
            t < count,
            jnp.where(r * n_col + row_at[t] == col_at[t] * n_col + c, 0.5, 1.0),
            0.0,
        ).astype(F32)
        for t in range(slots)
    ]

    def transpose(t):
        tiles_t[t] = tiles[t].T

    each(0, slots, transpose)
    forward(0)
    spread(0)
    weight_t = weight[...].T
    bias_t = jnp.broadcast_to(bias[...], (BLOCK, width)).T
    cotangent_t = cotangent[...].astype(F32).T
    mixed = collect(0, scaled)
    high = mixed.astype(BF16)
    low = (mixed - high.astype(F32)).astype(BF16)
    product = dot(weight_t, high) + dot(weight_t, low)
    preact = scale * product + bias_t
    sig = 1.0 / (1.0 + jnp.exp(-preact))
    delta = cotangent_t * sig * (1.0 + preact * (1.0 - sig))
    scaled_delta = (scale * delta).astype(BF16)
    gather(1, scaled_delta)

    local = dot(high, scaled_delta, ((1,), (1,)))
    local_bias = jnp.sum(delta.T, axis=0, keepdims=True)
    for k in range(n_row):
        w_part[k, :chunk, :] = local[k * chunk:(k + 1) * chunk]
        w_part[k, chunk:, :] = jnp.broadcast_to(local_bias, (8, width))
    each(1, n_row, lambda k: row_copy(4, k, w_part.at[row_peer(k)], w_in.at[r]).start())
    w_in[r] = w_part[r]
    act_ref[...] = (preact * sig).T.astype(BF16)
    store(0, act_ref, act_hbm)

    def sum_over_row():
        row_all(4, w_in).wait_recv()
        summed = w_in[0]
        for k in range(1, n_row):
            summed = summed + w_in[k]
        w_cross[c] = summed
        each(1, n_col, lambda k: col_copy(4, k, w_cross.at[c], w_cross.at[c]).start())

    forward(1)
    spread(1, sum_over_row)
    col_all(4, w_cross).wait_recv()
    summed = w_cross[0]
    for k in range(1, n_col):
        summed = summed + w_cross[k]
    w_all[r] = summed
    each(1, n_row, lambda k: row_copy(5, k, w_all.at[r], w_all.at[r]).start())
    bgrad_ref[...] = summed[chunk:chunk + 1]
    store(3, bgrad_ref, bgrad_hbm)

    proj_grad = (scale * collect(1, scaled_delta)).astype(BF16)
    fgrad_ref[...] = dot(weight[...], proj_grad).T.astype(BF16)
    store(1, fgrad_ref, fgrad_hbm)
    row_all(5, w_all).wait_recv()
    for k in range(n_row):
        wgrad_ref[k * chunk:(k + 1) * chunk, :] = w_all[k, :chunk, :]
    store(2, wgrad_ref, wgrad_hbm)
    for stage in range(2):
        mate_all(stage, x_col0).wait_send()
        sibling_all(stage, x_col0, chips).wait_send()
    for stage in range(2, 6):
        row_all(stage, x_col0 if stage < 4 else w_in).wait_send()
    for stage in range(5):
        col_all(stage, x_row0 if stage < 4 else w_cross).wait_send()
    for copy in stores:
        copy.wait()


def finish_kernel(count, *refs):
    sources, results, held = (refs[n * count:(n + 1) * count] for n in range(3))
    sem = refs[-1]
    fetches = [pltpu.make_async_copy(sources[n], held[n], sem.at[0, n]) for n in range(count)]
    stores = [pltpu.make_async_copy(held[n], results[n], sem.at[1, n]) for n in range(count)]
    for fetch in fetches:
        fetch.start()
    for n in range(count):
        fetches[n].wait()
        stores[n].start()
    for copy in stores:
        copy.wait()


def shards(
    n_row, n_col,
    features, weight, bias, node_scale, cotangent, tile_row, tile_col, tile_count, tile_values
):
    width = features.shape[1]
    slots = tile_row.shape[-1]
    assert features.shape[0] == BLOCK
    chunk = width // n_row
    hbm = pl.BlockSpec(memory_space=pltpu.HBM)
    shapes = (
        jax.ShapeDtypeStruct((BLOCK, width), BF16),
        jax.ShapeDtypeStruct((BLOCK, width), BF16),
        jax.ShapeDtypeStruct((width, width), F32),
        jax.ShapeDtypeStruct((1, width), F32),
    )
    results = pl.pallas_call(
        functools.partial(layer_kernel, n_row, n_col, slots),
        out_shape=shapes,
        in_specs=[hbm] * 9,
        out_specs=(hbm,) * 4,
        scratch_shapes=[pltpu.VMEM(shape.shape, shape.dtype) for shape in shapes]
        + [
            pltpu.SemaphoreType.DMA((4,)),
            pltpu.SMEM((slots,), jnp.int32),
            pltpu.SMEM((slots,), jnp.int32),
            pltpu.SMEM((1,), jnp.int32),
            pltpu.VMEM((BLOCK, width), BF16),
            pltpu.VMEM((width, width), BF16),
            pltpu.VMEM((1, width), F32),
            pltpu.VMEM((1, BLOCK), F32),
            pltpu.VMEM((BLOCK, width), BF16),
            pltpu.VMEM((slots, BLOCK, BLOCK), BF16),
            pltpu.VMEM((slots, BLOCK, BLOCK), BF16),
            pltpu.VMEM((slots, width, BLOCK), F32),
            pltpu.VMEM((2, n_col, width, BLOCK), BF16),
            pltpu.VMEM((2, n_row, width, BLOCK), BF16),
            pltpu.VMEM((2, n_col, width, BLOCK), BF16),
            pltpu.VMEM((2, n_row, width, BLOCK), BF16),
            pltpu.VMEM((n_row, chunk + 8, width), F32),
            pltpu.VMEM((n_row, chunk + 8, width), F32),
            pltpu.VMEM((n_col, chunk + 8, width), F32),
            pltpu.VMEM((n_row, chunk + 8, width), F32),
            pltpu.SemaphoreType.DMA((9,)),
            pltpu.SemaphoreType.DMA((6,)),
            pltpu.SemaphoreType.DMA((5,)),
            pltpu.SemaphoreType.DMA((6,)),
            pltpu.SemaphoreType.DMA((5,)),
            pltpu.SemaphoreType.DMA((2,)),
            pltpu.SemaphoreType.DMA((2,)),
            pltpu.VMEM((n_col, width, BLOCK), BF16),
            pltpu.VMEM((n_col, width, BLOCK), BF16),
            pltpu.VMEM((n_row, width, BLOCK), BF16),
            pltpu.VMEM((n_row, width, BLOCK), BF16),
        ],
        compiler_params=pltpu.CompilerParams(
            collective_id=0, has_side_effects=True, vmem_limit_bytes=VMEM_LIMIT
        ),
    )(
        tile_row.reshape(slots), tile_col.reshape(slots), tile_count.reshape(1),
        features, weight, bias.reshape(1, width), node_scale.reshape(1, BLOCK), cotangent,
        tile_values.reshape(slots, BLOCK, BLOCK),
    )
    act, fgrad, wgrad, bgrad = pl.pallas_call(
        functools.partial(finish_kernel, 4),
        out_shape=shapes,
        in_specs=[pl.BlockSpec(memory_space=pl.ANY)] * 4,
        out_specs=(hbm,) * 4,
        scratch_shapes=[pltpu.VMEM(shape.shape, shape.dtype) for shape in shapes]
        + [pltpu.SemaphoreType.DMA((2, 4))],
        compiler_params=pltpu.CompilerParams(vmem_limit_bytes=VMEM_LIMIT),
    )(*results)
    return act, fgrad, wgrad, bgrad.reshape(width)


def solution(mesh):
    placed = (
        P(("row", "col"), None),
        P(),
        P(),
        P(("row", "col")),
        P(("row", "col"), None),
        P("row", "col", None),
        P("row", "col", None),
        P("row", "col"),
        P("row", "col", None, None, None),
    )
    return jax.shard_map(
        functools.partial(shards, mesh.shape["row"], mesh.shape["col"]),
        mesh=mesh,
        in_specs=placed,
        out_specs=(P(("row", "col"), None), P(("row", "col"), None), P(), P()),
        check_vma=False,
    )
```
